32 devices in a mesh: mem: 4 (over z), reg: 8 (over y, x, core).
Axes of the slice: x: 2, y: 2, z: 4, core: 2. Of those that a mesh axis runs over, the one named last changes fastest.
Arguments:
- background: bfloat16 [240, 8, 4096], P('mem', 'reg'), may hold values from -6 to 6
- obs_index: int32 [8, 4, 512], P('reg'), may hold values from 0 to 1023
- yobs: bfloat16 [8, 4, 512], P('reg', 'mem'), may hold values from -6 to 6
- loc_list: int32 [8, 4, 2048], P('reg', 'mem'), may hold values from 0 to 4607, as said below
- loc_count: int32 [8, 4], P('reg', 'mem'), may hold values from 256 to 2048, as said below
- loc_weight: float32 [8, 4, 2048], P('reg', 'mem'), may hold values from 0.03 to 0.6
Outputs:
- analysis: bfloat16 [240, 8, 4096], P('mem', 'reg')
The draws below stay inside these ranges and needn't reach their ends.
Inputs may be any that keep to these rules, and one draw needn't show every extreme that they name: `loc_list`: for each region the first loc_count entries name distinct candidates; later entries are candidate numbers that carry no weight. `loc_count`: some region has exactly 2048 entries and some exactly 256.
All inputs are finite; a program needn't handle non-finite values.
Results may differ from the reference program's by a relative error of at most 0.006.
Values may be sent and summed in bfloat16 or wider, within the bound.
A program may use at most 64 MiB of HBM per device.

```python
import math
import jax
import jax.numpy as jnp
from jax import lax

K = 240
CELLS = 1024
OBS_REG = 512
LMAX = 2048
NS_STEPS = 5
COLS = 8
ROWS = 4


def draw_loc_list(key, part):
    base_key = jax.random.fold_in(key, 11)
    region_keys = jax.random.split(base_key, COLS * ROWS)

    def one_list(subkey):
        return jax.random.permutation(subkey, 9 * OBS_REG)[:LMAX]
    lists = jax.vmap(one_list)(region_keys)
    return lists.reshape(COLS, ROWS, LMAX).astype(jnp.int32)


def draw_loc_count(key, part):
    base_key = jax.random.fold_in(key, 23)
    key_excess, key_top, key_least = jax.random.split(base_key, 3)
    region_total = COLS * ROWS
    least_count = LMAX // 8
    spread_range = LMAX - least_count
    excess = jax.random.randint(key_excess, (region_total,), 0, spread_range + 1)
    counts = least_count + excess * excess // spread_range
    top_position = jax.random.randint(key_top, (), 0, region_total)
    least_position = (top_position + 1 + jax.random.randint(key_least, (), 0, region_total - 1)) % region_total
    positions = jnp.arange(region_total, dtype=jnp.int32)
    counts = jnp.where(positions == top_position, LMAX, counts)
    counts = jnp.where(positions == least_position, least_count, counts)
    return counts.reshape(COLS, ROWS).astype(jnp.int32)


def plant(result, key, low, high):
    spot = [jax.random.randint(jax.random.fold_in(key, axis), (), 0, length) for axis, length in enumerate(result.shape)]
    main_axis = result.shape.index(max(result.shape))
    next_to = spot[:main_axis] + [(spot[main_axis] + 1) % result.shape[main_axis]] + spot[main_axis + 1:]
    return result.at[tuple(spot)].set(low).at[tuple(next_to)].set(high)


def block_levels(key, extent, cuts, least, largest):
    gain = 1.0
    for dim, parts in cuts:
        draws = jax.random.uniform(jax.random.fold_in(jax.random.fold_in(key, 6), dim), (parts,), jnp.float32, least / len(cuts), largest / len(cuts))
        gain = gain * jnp.repeat(jnp.exp(draws), extent[dim] // parts).reshape((-1,) + (1,) * (len(extent) - 1 - dim))
    return gain


def scatter_about(own_key, shape, width, reach, shards=(), held_as=jnp.bfloat16):
    values = jax.random.normal(own_key, shape, jnp.float32) * width
    if len(shards) > 0:
        values = block_levels(own_key, shape, shards, -0.22, 0.18) * values
    return jnp.clip(values, min=-reach, max=reach).astype(held_as)


def setup_inputs(seed: int = 0) -> dict:
    arg_keys = jax.random.split(jax.random.key(seed), 7)
    background = scatter_about(arg_keys[0], (K, COLS, ROWS * CELLS), 1.0, 6.0, ((0, 4), (1, 8)))
    obs_index = plant(jax.random.randint(arg_keys[1], (COLS, ROWS, OBS_REG), 0, CELLS), jax.random.fold_in(arg_keys[1], 1), 0, CELLS - 1).astype(jnp.int32)
    yobs = scatter_about(arg_keys[2], (COLS, ROWS, OBS_REG), 1.0, 6.0, ((0, 8), (1, 4)))
    loc_list = draw_loc_list(jax.random.fold_in(arg_keys[6], 71), 0)
    loc_count = draw_loc_count(jax.random.fold_in(arg_keys[6], 71), 0)
    loc_weight = jnp.clip(jnp.exp(math.log(0.6) - 2.9957323 * jax.random.uniform(arg_keys[5], (COLS, ROWS, LMAX), jnp.float32) ** block_levels(arg_keys[5], (COLS, ROWS, LMAX), ((0, 8), (1, 4)), -0.2, 0.2)), 0.03, 0.6)
    return dict(background=background, obs_index=obs_index, yobs=yobs, loc_list=loc_list, loc_count=loc_count, loc_weight=loc_weight)


inflation = 1.1

def newton_root(gram_matrix):
    size = gram_matrix.shape[0]
    identity = jnp.eye(size, dtype=jnp.float32)
    norm_value = jnp.sqrt(jnp.sum(gram_matrix * gram_matrix))
    current = gram_matrix / norm_value
    inverse_root = identity
    for iteration in range(NS_STEPS):
        correction = 1.5 * identity - 0.5 * jnp.dot(inverse_root, current, precision=lax.Precision.HIGHEST)
        current = jnp.dot(current, correction, precision=lax.Precision.HIGHEST)
        inverse_root = jnp.dot(correction, inverse_root, precision=lax.Precision.HIGHEST)
    return (inverse_root, norm_value)

def analyze(own_state, candidates, obs_order, obs_count, obs_taper):
    members = own_state.shape[0]
    state_mean = lax.optimization_barrier(jnp.sum(own_state.astype(jnp.float32), axis=0)) / members
    state_pert = (own_state.astype(jnp.float32) - state_mean).astype(jnp.bfloat16)
    ensemble = candidates[:members].astype(jnp.float32)
    obs_mean = lax.optimization_barrier(jnp.sum(ensemble, axis=0)) / members
    obs_pert = (ensemble - obs_mean).astype(jnp.bfloat16)
    innovation = (candidates[members].astype(jnp.float32) - obs_mean).astype(jnp.bfloat16)
    local_pert = jnp.take(obs_pert, obs_order, axis=1)
    local_innov = jnp.take(innovation, obs_order)
    positions = jnp.arange(obs_order.shape[0], dtype=jnp.int32)
    live_weight = jnp.where(positions < obs_count, obs_taper, jnp.float32(0.0))
    weighted = (local_pert.astype(jnp.float32) * live_weight).astype(jnp.bfloat16)
    gram_matrix = jnp.dot(weighted, local_pert.T, preferred_element_type=jnp.float32)
    drive_vector = jnp.dot(weighted, local_innov, preferred_element_type=jnp.float32)
    gram_matrix = gram_matrix + (members - 1) / inflation * jnp.eye(members, dtype=jnp.float32)
    inverse_root, norm_value = newton_root(gram_matrix)
    mean_shift = jnp.dot(inverse_root, jnp.dot(inverse_root, drive_vector, precision=lax.Precision.HIGHEST), precision=lax.Precision.HIGHEST)
    weights = math.sqrt(members - 1) / jnp.sqrt(norm_value) * inverse_root + (mean_shift / norm_value)[:, None]
    weights = weights.astype(jnp.bfloat16)
    update = jnp.dot(weights.T, state_pert, preferred_element_type=jnp.float32)
    return (state_mean + update).astype(jnp.bfloat16)

def reference(background, obs_index, yobs, loc_list, loc_count, loc_weight):
    states = background.reshape(K, COLS, ROWS, CELLS)

    def one_region(flat_index):
        column = flat_index // ROWS
        row_index = flat_index % ROWS
        pieces = []
        for offset_col in range(3):
            for offset_row in range(3):
                source_col = (column + offset_col - 1) % COLS
                source_row = (row_index + offset_row - 1) % ROWS
                cells_here = states[:, source_col, source_row, :]
                picked = jnp.take(cells_here, obs_index[source_col, source_row], axis=1)
                pieces.append(jnp.concatenate([picked, yobs[source_col, source_row][None, :]], axis=0))
        candidates = jnp.concatenate(pieces, axis=1)
        return analyze(states[:, column, row_index, :], candidates, loc_list[column, row_index], loc_count[column, row_index], loc_weight[column, row_index])
    regions = lax.map(one_region, jnp.arange(COLS * ROWS, dtype=jnp.int32))
    return regions.reshape(COLS, ROWS, K, CELLS).transpose(2, 0, 1, 3).reshape(K, COLS, ROWS * CELLS)
```

```python
import functools
import math

import jax
import jax.numpy as jnp
from jax import lax
from jax.experimental import pallas as pl
from jax.experimental.pallas import tpu as pltpu
from jax.sharding import PartitionSpec as P

NS_STEPS = 5
INFLATION = 1.1
MESH = pl.DeviceIdType.MESH
F32 = jnp.float32
BF16 = jnp.bfloat16


def split(x):
    high = x.astype(BF16)
    return high, (x - high.astype(F32)).astype(BF16)


def mm(a, b):
    return (
        jnp.dot(a[0], b[1], preferred_element_type=F32)
        + jnp.dot(a[1], b[0], preferred_element_type=F32)
        + jnp.dot(a[0], b[0], preferred_element_type=F32)
    )


def dot_t(a, b):
    return lax.dot_general(a, b, (((1,), (1,)), ((), ())), preferred_element_type=F32)


def newton(gram, norm, eye, steps):
    current = gram * (1.0 / norm)
    root = None
    for step in range(steps):
        last = step == steps - 1
        if root is None:
            corr = 1.5 * eye - 0.5 * current
            corr_s = split(corr)
            root = corr
        else:
            cur_s, root_s = split(current), split(root)
            corr = 1.5 * eye - 0.5 * mm(root_s, cur_s)
            corr_s = split(corr)
            root = mm(corr_s, root_s)
        if not last:
            current = mm(split(current), corr_s)
    return root


def kernel(
    n, regs, m, pad, width, cells,
    bg_ref, idx_ref, yobs_ref, list_ref, count_ref, weight_ref,
    out_ref,
    bgp, obs_loc, obuf, sbuf, wd, wbuf, yloc, ybuf, pert, gsend, grecv, wt, oloc,
    obs_ss, obs_rs, st_ss, st_rs, w_ss, w_rs, y_ss, y_rs, g_ss, g_rs, o_ss, o_rs,
):
    me, col = lax.axis_index("mem"), lax.axis_index("reg")
    left, right = lax.rem(col + regs - 1, regs), lax.rem(col + 1, regs)
    members, total = n * m, n * pad
    lanes = 128
    strips = width // lanes
    block = wd.shape[0] // 3

    def peer(d):
        return lax.rem(me + d, n)

    barrier = pltpu.get_barrier_semaphore()
    for d in range(1, n):
        pl.semaphore_signal(barrier, inc=1, device_id=(peer(d), col), device_id_type=MESH)
    for c in (left, right):
        pl.semaphore_signal(barrier, inc=1, device_id=(me, c), device_id_type=MESH)

    def send(src, dst, ss, rs, device):
        copy = pltpu.make_async_remote_copy(
            src_ref=src, dst_ref=dst, send_sem=ss, recv_sem=rs,
            device_id=device, device_id_type=MESH,
        )
        copy.start()
        return copy

    tail = (m // 16) * 16
    for q in range(n):
        bgp[q, tail:pad, :] = jnp.zeros((pad - tail, cells), BF16)
        bgp[q, 0:m, :] = bg_ref[:, q * cells:(q + 1) * cells]

    length = list_ref.shape[1]
    place = lax.broadcasted_iota(jnp.int32, (1, length), 1)
    live = jnp.where(place < count_ref[...], weight_ref[...], 0.0)
    part0 = live.astype(BF16)
    rest = live - part0.astype(F32)
    part1 = rest.astype(BF16)
    part2 = (rest - part1.astype(F32)).astype(BF16)
    cand = list_ref[...]
    strip = cand // lanes
    lane = cand - strip * lanes
    group = strip // (3 * strips)
    strip = strip + group * (block - 3 * strips)
    rows_at = lax.broadcasted_iota(jnp.int32, (3 * block, length), 0) == strip
    lanes_at = lax.broadcasted_iota(jnp.int32, (lanes, length), 0) == lane
    lane_hot = jnp.where(lanes_at, 1.0, 0.0).astype(BF16)
    spread = [
        dot_t(jnp.where(rows_at, part.astype(F32), 0.0).astype(BF16), lane_hot)
        for part in (part0, part1, part2)
    ]
    wd[...] = spread[0] + (spread[1] + spread[2])
    yloc[...] = jnp.broadcast_to(yobs_ref[...].astype(F32), yloc.shape)
    ybuf[1] = yloc[...]

    pl.semaphore_wait(barrier, n + 1)

    copies = []
    w_left = send(wd.at[pl.ds(0, block)], wbuf.at[0], w_ss.at[0], w_rs.at[0], (me, left))
    w_right = send(wd.at[pl.ds(2 * block, block)], wbuf.at[1], w_ss.at[1], w_rs.at[1], (me, right))
    y_up = send(yloc, ybuf.at[0], y_ss.at[0], y_rs.at[0], (peer(1), col))
    y_down = send(yloc, ybuf.at[2], y_ss.at[1], y_rs.at[1], (peer(n - 1), col))

    order = sorted(range(n), key=lambda t: -min(t, n - t))
    obs_copies = []
    for t in order:
        row = peer(t)
        hot = lax.broadcasted_iota(jnp.int32, (cells, width), 0) == idx_ref[pl.ds(row, 1), :]
        hot = jnp.where(hot, 1.0, 0.0).astype(BF16)
        obs_loc[t] = jnp.dot(bgp[row], hot, preferred_element_type=F32).astype(BF16)
        for slot in (0, 1, 2):
            d = (t + 1 - slot) % n
            if d == 0:
                obuf[me, slot] = obs_loc[t]
            else:
                obs_copies.append(
                    send(obs_loc.at[t], obuf.at[me, slot], obs_ss.at[d, slot], obs_rs.at[d, slot], (peer(d), col))
                )
    for copy in obs_copies:
        copy.wait_recv()

    state_copies = []
    for d in range(n - 1, 0, -1):
        state_copies.append(
            send(bgp.at[peer(d)], sbuf.at[me], st_ss.at[d], st_rs.at[d], (peer(d), col))
        )
    sbuf[me] = bgp[me]

    y_up.wait_recv()
    y_down.wait_recv()
    row_id = lax.broadcasted_iota(jnp.int32, (total, 1), 0)
    real = lax.rem(row_id, pad) < m
    for slot in range(3):
        seen = obuf[:, slot].reshape(total, width).astype(F32)
        mean = jnp.sum(seen, axis=0, keepdims=True) / members
        innov = ybuf[slot][0:1, :] - mean
        values = jnp.where(real, seen - mean, jnp.where(row_id == m, innov, 0.0))
        pert[slot] = values.astype(BF16)

    def gram_of(weights):
        acc = None
        for slot in range(3):
            strip_rows = [weights[slot * strips + i:slot * strips + i + 1, :] for i in range(strips)]
            scale = jnp.concatenate(strip_rows, axis=1)
            values = pert[slot]
            weighted = (values.astype(F32) * scale).astype(BF16)
            term = dot_t(weighted, values)
            acc = term if acc is None else acc + term
        return acc

    w_left.wait_recv()
    gsend[0] = gram_of(wbuf[0]).astype(BF16)
    g_right = send(gsend.at[0], grecv.at[0], g_ss.at[0], g_rs.at[0], (me, right))
    w_right.wait_recv()
    gsend[1] = gram_of(wbuf[1]).astype(BF16)
    g_left = send(gsend.at[1], grecv.at[1], g_ss.at[1], g_rs.at[1], (me, left))
    own = gram_of(wd[block:2 * block, :])
    g_right.wait_recv()
    g_left.wait_recv()
    full = own + (grecv[0].astype(F32) + grecv[1].astype(F32))

    col_id = lax.broadcasted_iota(jnp.int32, (1, total), 1)
    real_col = lax.rem(col_id, pad) < m
    same = row_id == col_id
    eye = jnp.where(same, 1.0, 0.0)
    drive = jnp.where(real_col, full[m:m + 1, :], 0.0)
    gram = jnp.where(real & real_col, full, 0.0)
    gram = gram + jnp.where(same & real, (members - 1) / INFLATION, 0.0)
    norm = jnp.sqrt(jnp.sum(jnp.sum(gram * gram, axis=0, keepdims=True), axis=1, keepdims=True))
    root = newton(gram, norm, eye, NS_STEPS)
    inner = jnp.sum(root * drive, axis=1, keepdims=True)
    shift = jnp.sum(root * inner, axis=0, keepdims=True)
    wt[...] = (math.sqrt(members - 1) / jnp.sqrt(norm) * root + shift / norm).astype(BF16)

    for copy in state_copies:
        copy.wait_recv()
    states = sbuf[...].reshape(total, cells).astype(F32)
    state_mean = jnp.sum(states, axis=0, keepdims=True) / members
    state_pert = jnp.where(real, states - state_mean, 0.0).astype(BF16)

    mine = pl.ds(pl.multiple_of(me * cells, 128), cells)
    out_copies = []
    for d in list(range(n - 1, 0, -1)) + [0]:
        dest = peer(d)
        rows = wt[pl.ds(pl.multiple_of(dest * pad, 16), pad), :]
        result = (state_mean + jnp.dot(rows, state_pert, preferred_element_type=F32)).astype(BF16)
        if d == 0:
            out_ref[:, mine] = result
        else:
            oloc[d] = result
            out_copies.append(
                send(oloc.at[d], out_ref.at[:, mine], o_ss.at[d], o_rs.at[d], (dest, col))
            )
    for copy in out_copies:
        copy.wait_recv()
    for copy in obs_copies + state_copies + out_copies:
        copy.wait_send()
    for copy in (w_left, w_right, y_up, y_down, g_right, g_left):
        copy.wait_send()


def local(background, obs_index, yobs, loc_list, loc_count, loc_weight):
    n, regs = lax.axis_size("mem"), lax.axis_size("reg")
    m = background.shape[0]
    rows, width = obs_index.shape[1], obs_index.shape[2]
    cells = background.shape[2] // rows
    length = loc_list.shape[2]
    pad = (m // 16 + 1) * 16
    total = n * pad
    block = -(-3 * (width // 128) // 8) * 8
    vmem = pl.BlockSpec(memory_space=pltpu.VMEM)
    dma = pltpu.SemaphoreType.DMA
    result = pl.pallas_call(
        functools.partial(kernel, n, regs, m, pad, width, cells),
        out_shape=jax.ShapeDtypeStruct((pad, rows * cells), BF16),
        in_specs=[vmem] * 6,
        out_specs=vmem,
        scratch_shapes=[
            pltpu.VMEM((n, pad, cells), BF16),
            pltpu.VMEM((n, pad, width), BF16),
            pltpu.VMEM((n, 3, pad, width), BF16),
            pltpu.VMEM((n, pad, cells), BF16),
            pltpu.VMEM((3 * block, 128), F32),
            pltpu.VMEM((2, block, 128), F32),
            pltpu.VMEM((8, width), F32),
            pltpu.VMEM((3, 8, width), F32),
            pltpu.VMEM((3, total, width), BF16),
            pltpu.VMEM((2, total, total), BF16),
            pltpu.VMEM((2, total, total), BF16),
            pltpu.VMEM((total, total), BF16),
            pltpu.VMEM((n, pad, cells), BF16),
            dma((n, 3)), dma((n, 3)),
            dma((n,)), dma((n,)),
            dma((2,)), dma((2,)),
            dma((2,)), dma((2,)),
            dma((2,)), dma((2,)),
            dma((n,)), dma((n,)),
        ],
        compiler_params=pltpu.CompilerParams(
            collective_id=0, has_side_effects=True, vmem_limit_bytes=40 * 1024 * 1024
        ),
    )(
        background.reshape(m, rows * cells),
        obs_index.reshape(rows, width),
        yobs.reshape(1, width),
        loc_list.reshape(1, length),
        loc_count.reshape(1, 1),
        loc_weight.reshape(1, length),
    )
    return result[:m].reshape(m, 1, rows * cells)


def solution(mesh):
    return jax.shard_map(
        local,
        mesh=mesh,
        in_specs=(
            P("mem", "reg", None),
            P("reg", None, None),
            P("reg", "mem", None),
            P("reg", "mem", None),
            P("reg", "mem"),
            P("reg", "mem", None),
        ),
        out_specs=P("mem", "reg", None),
        check_vma=False,
    )
```

```python
import functools
import math

import jax
import jax.numpy as jnp
from jax import lax
from jax.experimental import pallas as pl
from jax.experimental.pallas import tpu as pltpu
from jax.sharding import PartitionSpec as P

NS_STEPS = 5
INFLATION = 1.1
MESH = pl.DeviceIdType.MESH
F32 = jnp.float32
BF16 = jnp.bfloat16


def split(x):
    high = x.astype(BF16)
    return high, (x - high.astype(F32)).astype(BF16)


def mm(a, b):
    return (
        jnp.dot(a[0], b[1], preferred_element_type=F32)
        + jnp.dot(a[1], b[0], preferred_element_type=F32)
        + jnp.dot(a[0], b[0], preferred_element_type=F32)
    )


def dot_t(a, b):
    return lax.dot_general(a, b, (((1,), (1,)), ((), ())), preferred_element_type=F32)


def newton(gram, norm, eye, steps):
    current = gram * (1.0 / norm)
    root = None
    for step in range(steps):
        last = step == steps - 1
        if root is None:
            corr = 1.5 * eye - 0.5 * current
            corr_s = split(corr)
            root = corr
        else:
            cur_s, root_s = split(current), split(root)
            corr = 1.5 * eye - 0.5 * mm(root_s, cur_s)
            corr_s = split(corr)
            root = mm(corr_s, root_s)
        if not last:
            current = mm(split(current), corr_s)
    return root


def kernel(
    n, regs, m, pad, width, cells,
    bg_hbm, idx_hbm, yobs_hbm, list_hbm, count_hbm, weight_hbm,
    out_ref,
    bg_ref, idx_ref, yobs_ref, list_ref, count_ref, weight_ref,
    bgp, obs_loc, obuf, sbuf, wd, wbuf, yloc, ybuf, pert, gsend, grecv, wt, oloc,
    obs_ss, obs_rs, st_ss, st_rs, w_ss, w_rs, y_ss, y_rs, g_ss, g_rs, o_ss, o_rs, in_sem,
):
    me, col = lax.axis_index("mem"), lax.axis_index("reg")
    left, right = lax.rem(col + regs - 1, regs), lax.rem(col + 1, regs)
    members, total = n * m, n * pad
    lanes = 128
    strips = width // lanes
    block = wd.shape[0] // 3

    def peer(d):
        return lax.rem(me + d, n)

    barrier = pltpu.get_barrier_semaphore()
    for d in range(1, n):
        pl.semaphore_signal(barrier, inc=1, device_id=(peer(d), col), device_id_type=MESH)
    for c in (left, right):
        pl.semaphore_signal(barrier, inc=1, device_id=(me, c), device_id_type=MESH)

    def send(src, dst, ss, rs, device):
        copy = pltpu.make_async_remote_copy(
            src_ref=src, dst_ref=dst, send_sem=ss, recv_sem=rs,
            device_id=device, device_id_type=MESH,
        )
        copy.start()
        return copy

    loads = [
        pltpu.make_async_copy(src, dst, in_sem.at[i])
        for i, (src, dst) in enumerate((
            (bg_hbm, bg_ref), (idx_hbm, idx_ref), (yobs_hbm, yobs_ref),
            (list_hbm, list_ref), (count_hbm, count_ref), (weight_hbm, weight_ref),
        ))
    ]
    for load in loads:
        load.start()
    for load in loads[2:]:
        load.wait()

    length = list_ref.shape[1]
    place = lax.broadcasted_iota(jnp.int32, (1, length), 1)
    live = jnp.where(place < count_ref[...], weight_ref[...], 0.0)
    part0 = live.astype(BF16)
    rest = live - part0.astype(F32)
    part1 = rest.astype(BF16)
    part2 = (rest - part1.astype(F32)).astype(BF16)
    cand = list_ref[...]
    strip = cand // lanes
    lane = cand - strip * lanes
    group = strip // (3 * strips)
    strip = strip + group * (block - 3 * strips)
    rows_at = lax.broadcasted_iota(jnp.int32, (3 * block, length), 0) == strip
    lanes_at = lax.broadcasted_iota(jnp.int32, (lanes, length), 0) == lane
    lane_hot = jnp.where(lanes_at, 1.0, 0.0).astype(BF16)
    spread = [
        dot_t(jnp.where(rows_at, part.astype(F32), 0.0).astype(BF16), lane_hot)
        for part in (part0, part1, part2)
    ]
    wd[...] = spread[0] + (spread[1] + spread[2])
    yloc[...] = jnp.broadcast_to(yobs_ref[...].astype(F32), yloc.shape)
    ybuf[1] = yloc[...]

    loads[0].wait()
    loads[1].wait()
    tail = (m // 16) * 16
    for q in range(n):
        bgp[q, tail:pad, :] = jnp.zeros((pad - tail, cells), BF16)
        bgp[q, 0:m, :] = bg_ref[:, q * cells:(q + 1) * cells]

    pl.semaphore_wait(barrier, n + 1)

    copies = []
    w_left = send(wd.at[pl.ds(0, block)], wbuf.at[0], w_ss.at[0], w_rs.at[0], (me, left))
    w_right = send(wd.at[pl.ds(2 * block, block)], wbuf.at[1], w_ss.at[1], w_rs.at[1], (me, right))
    y_up = send(yloc, ybuf.at[0], y_ss.at[0], y_rs.at[0], (peer(1), col))
    y_down = send(yloc, ybuf.at[2], y_ss.at[1], y_rs.at[1], (peer(n - 1), col))

    def observe(row):
        hot = lax.broadcasted_iota(jnp.int32, (cells, width), 0) == idx_ref[pl.ds(row, 1), :]
        hot = jnp.where(hot, 1.0, 0.0).astype(BF16)
        return jnp.dot(bgp[row], hot, preferred_element_type=F32).astype(BF16)

    obs_copies = []
    if n == 4:
        side = me // 2

        def turn(x, last):
            return x + side * (last - 2 * x)

        here = turn(me, 3)
        inner = here == 1
        other = 1 - here

        def obs_send(row, dest, slot, i):
            return send(
                obs_loc.at[row], obuf.at[me, turn(slot, 2)], obs_ss.at[i],
                obs_rs.at[me, turn(slot, 2)], (turn(dest, 3), col),
            )

        def landed(source, slot):
            return pltpu.make_async_remote_copy(
                src_ref=obs_loc.at[0], dst_ref=obuf.at[turn(source, 3), turn(slot, 2)],
                send_sem=obs_ss.at[0], recv_sem=obs_rs.at[turn(source, 3), turn(slot, 2)],
                device_id=(turn(other, 3), col), device_id_type=MESH,
            )

        for i, (row, dest, slot) in enumerate(((2, 2, 1), (3, 2, 2), (1, 2, 0), (0, 3, 2))):
            obs_loc[row] = observe(turn(row, 3))
            obs_copies.append(obs_send(row, dest, slot, i))
        for slot in range(3):
            obs_copies.append(obs_send(lax.rem(other + slot + 3, 4), other, slot, 4 + slot))
        for slot in range(3):
            obuf[me, turn(slot, 2)] = obs_loc[lax.rem(here + slot + 3, 4)]

        handed = ((2, 1), (2, 0), (3, 1), (3, 0))

        def hand_on(i, source, slot):
            return pltpu.make_async_remote_copy(
                src_ref=obuf.at[turn(source, 3), turn(slot, 2)],
                dst_ref=obuf.at[turn(source, 3), turn(slot + 1, 2)],
                send_sem=obs_ss.at[7 + i], recv_sem=obs_rs.at[turn(source, 3), turn(slot + 1, 2)],
                device_id=(turn(0, 3), col), device_id_type=MESH,
            )

        @pl.when(inner)
        def _():
            for i, (source, slot) in enumerate(handed):
                landed(source, slot).wait_recv()
                hand_on(i, source, slot).start()
            for source in (2, 3):
                landed(source, 2).wait_recv()

        @pl.when(jnp.logical_not(inner))
        def _():
            for source in (2, 3):
                for slot in range(3):
                    landed(source, slot).wait_recv()

        for slot in range(3):
            landed(other, slot).wait_recv()
    else:
        for t in sorted(range(n), key=lambda t: -min(t, n - t)):
            obs_loc[t] = observe(peer(t))
            for slot in (0, 1, 2):
                d = (t + 1 - slot) % n
                if d == 0:
                    obuf[me, slot] = obs_loc[t]
                else:
                    obs_copies.append(
                        send(
                            obs_loc.at[t], obuf.at[me, slot], obs_ss.at[3 * d + slot],
                            obs_rs.at[d, slot], (peer(d), col),
                        )
                    )
        for copy in obs_copies:
            copy.wait_recv()

    state_copies = []
    for d in range(n - 1, 0, -1):
        state_copies.append(
            send(bgp.at[peer(d)], sbuf.at[me], st_ss.at[d], st_rs.at[d], (peer(d), col))
        )
    sbuf[me] = bgp[me]

    y_up.wait_recv()
    y_down.wait_recv()
    row_id = lax.broadcasted_iota(jnp.int32, (total, 1), 0)
    real = lax.rem(row_id, pad) < m
    for slot in range(3):
        seen = obuf[:, slot].reshape(total, width).astype(F32)
        mean = jnp.sum(seen, axis=0, keepdims=True) / members
        innov = ybuf[slot][0:1, :] - mean
        values = jnp.where(real, seen - mean, jnp.where(row_id == m, innov, 0.0))
        pert[slot] = values.astype(BF16)

    def gram_of(weights):
        acc = None
        for slot in range(3):
            strip_rows = [weights[slot * strips + i:slot * strips + i + 1, :] for i in range(strips)]
            scale = jnp.concatenate(strip_rows, axis=1)
            values = pert[slot]
            weighted = (values.astype(F32) * scale).astype(BF16)
            term = dot_t(weighted, values)
            acc = term if acc is None else acc + term
        return acc

    w_left.wait_recv()
    gsend[0] = gram_of(wbuf[0]).astype(BF16)
    g_right = send(gsend.at[0], grecv.at[0], g_ss.at[0], g_rs.at[0], (me, right))
    w_right.wait_recv()
    gsend[1] = gram_of(wbuf[1]).astype(BF16)
    g_left = send(gsend.at[1], grecv.at[1], g_ss.at[1], g_rs.at[1], (me, left))
    own = gram_of(wd[block:2 * block, :])
    g_right.wait_recv()
    g_left.wait_recv()
    full = own + (grecv[0].astype(F32) + grecv[1].astype(F32))

    col_id = lax.broadcasted_iota(jnp.int32, (1, total), 1)
    real_col = lax.rem(col_id, pad) < m
    same = row_id == col_id
    eye = jnp.where(same, 1.0, 0.0)
    drive = jnp.where(real_col, full[m:m + 1, :], 0.0)
    gram = jnp.where(real & real_col, full, 0.0)
    gram = gram + jnp.where(same & real, (members - 1) / INFLATION, 0.0)
    norm = jnp.sqrt(jnp.sum(jnp.sum(gram * gram, axis=0, keepdims=True), axis=1, keepdims=True))
    root = newton(gram, norm, eye, NS_STEPS)
    product = jnp.sum(root * drive, axis=1, keepdims=True)
    shift = jnp.sum(root * product, axis=0, keepdims=True)
    wt[...] = (math.sqrt(members - 1) / jnp.sqrt(norm) * root + shift / norm).astype(BF16)

    for copy in state_copies:
        copy.wait_recv()
    states = sbuf[...].reshape(total, cells).astype(F32)
    state_mean = jnp.sum(states, axis=0, keepdims=True) / members
    state_pert = jnp.where(real, states - state_mean, 0.0).astype(BF16)

    mine = pl.ds(pl.multiple_of(me * cells, 128), cells)
    out_copies = []
    for d in list(range(n - 1, 0, -1)) + [0]:
        dest = peer(d)
        rows = wt[pl.ds(pl.multiple_of(dest * pad, 16), pad), :]
        result = (state_mean + jnp.dot(rows, state_pert, preferred_element_type=F32)).astype(BF16)
        if d == 0:
            out_ref[:, mine] = result
        else:
            oloc[d] = result
            out_copies.append(
                send(oloc.at[d], out_ref.at[:, mine], o_ss.at[d], o_rs.at[d], (dest, col))
            )
    for copy in out_copies:
        copy.wait_recv()
    for copy in obs_copies + state_copies + out_copies:
        copy.wait_send()
    for copy in (w_left, w_right, y_up, y_down, g_right, g_left):
        copy.wait_send()
    if n == 4:
        @pl.when(inner)
        def _():
            for i, (source, slot) in enumerate(handed):
                hand_on(i, source, slot).wait_send()


def local(background, obs_index, yobs, loc_list, loc_count, loc_weight):
    n, regs = lax.axis_size("mem"), lax.axis_size("reg")
    m = background.shape[0]
    rows, width = obs_index.shape[1], obs_index.shape[2]
    cells = background.shape[2] // rows
    length = loc_list.shape[2]
    pad = (m // 16 + 1) * 16
    total = n * pad
    block = -(-3 * (width // 128) // 8) * 8
    vmem = pl.BlockSpec(memory_space=pltpu.VMEM)
    dma = pltpu.SemaphoreType.DMA
    result = pl.pallas_call(
        functools.partial(kernel, n, regs, m, pad, width, cells),
        out_shape=jax.ShapeDtypeStruct((pad, rows * cells), BF16),
        in_specs=[pl.BlockSpec(memory_space=pltpu.HBM)] * 6,
        out_specs=vmem,
        scratch_shapes=[
            pltpu.VMEM((m, rows * cells), BF16),
            pltpu.VMEM((rows, width), jnp.int32),
            pltpu.VMEM((1, width), BF16),
            pltpu.VMEM((1, length), jnp.int32),
            pltpu.VMEM((1, 1), jnp.int32),
            pltpu.VMEM((1, length), F32),
            pltpu.VMEM((n, pad, cells), BF16),
            pltpu.VMEM((n, pad, width), BF16),
            pltpu.VMEM((n, 3, pad, width), BF16),
            pltpu.VMEM((n, pad, cells), BF16),
            pltpu.VMEM((3 * block, 128), F32),
            pltpu.VMEM((2, block, 128), F32),
            pltpu.VMEM((8, width), F32),
            pltpu.VMEM((3, 8, width), F32),
            pltpu.VMEM((3, total, width), BF16),
            pltpu.VMEM((2, total, total), BF16),
            pltpu.VMEM((2, total, total), BF16),
            pltpu.VMEM((total, total), BF16),
            pltpu.VMEM((n, pad, cells), BF16),
            dma((3 * n,)), dma((n, 3)),
            dma((n,)), dma((n,)),
            dma((2,)), dma((2,)),
            dma((2,)), dma((2,)),
            dma((2,)), dma((2,)),
            dma((n,)), dma((n,)), dma((6,)),
        ],
        compiler_params=pltpu.CompilerParams(
            collective_id=0, has_side_effects=True, vmem_limit_bytes=40 * 1024 * 1024
        ),
    )(
        background.reshape(m, rows * cells),
        obs_index.reshape(rows, width),
        yobs.reshape(1, width),
        loc_list.reshape(1, length),
        loc_count.reshape(1, 1),
        loc_weight.reshape(1, length),
    )
    return result[:m].reshape(m, 1, rows * cells)


def solution(mesh):
    return jax.shard_map(
        local,
        mesh=mesh,
        in_specs=(
            P("mem", "reg", None),
            P("reg", None, None),
            P("reg", "mem", None),
            P("reg", "mem", None),
            P("reg", "mem"),
            P("reg", "mem", None),
        ),
        out_specs=P("mem", "reg", None),
        check_vma=False,
    )
```

```python
import functools
import math

import jax
import jax.numpy as jnp
from jax import lax
from jax.experimental import pallas as pl
from jax.experimental.pallas import tpu as pltpu
from jax.sharding import PartitionSpec as P

NS_STEPS = 5
INFLATION = 1.1
MESH = pl.DeviceIdType.MESH
F32 = jnp.float32
BF16 = jnp.bfloat16


def split(x):
    high = x.astype(BF16)
    return high, (x - high.astype(F32)).astype(BF16)


def mm(a, b):
    return (
        jnp.dot(a[0], b[1], preferred_element_type=F32)
        + jnp.dot(a[1], b[0], preferred_element_type=F32)
        + jnp.dot(a[0], b[0], preferred_element_type=F32)
    )


def dot_t(a, b):
    return lax.dot_general(a, b, (((1,), (1,)), ((), ())), preferred_element_type=F32)


def newton(gram, norm, eye, steps):
    current = gram * (1.0 / norm)
    root = None
    for step in range(steps):
        last = step == steps - 1
        if root is None:
            corr = 1.5 * eye - 0.5 * current
            corr_s = split(corr)
            root = corr
        else:
            cur_s, root_s = split(current), split(root)
            corr = 1.5 * eye - 0.5 * mm(root_s, cur_s)
            corr_s = split(corr)
            root = mm(corr_s, root_s)
        if not last:
            current = mm(split(current), corr_s)
    return root


def kernel(
    n, regs, m, pad, width, cells,
    bg_hbm, idx_hbm, yobs_hbm, list_hbm, count_hbm, weight_hbm,
    out_ref,
    bg_ref, idx_ref, yobs_ref, list_ref, count_ref, weight_ref,
    bgp, obs_loc, obuf, sbuf, wd, wbuf, yloc, ybuf, gacc, gsend, grecv, wt, oloc,
    obs_ss, obs_rs, st_ss, st_rs, w_ss, w_rs, y_ss, y_rs, g_ss, g_rs, o_ss, o_rs, in_sem,
):
    me, col = lax.axis_index("mem"), lax.axis_index("reg")
    left, right = lax.rem(col + regs - 1, regs), lax.rem(col + 1, regs)
    members, total = n * m, n * pad
    lanes = 128
    strips = width // lanes
    block = wd.shape[0] // 3

    def peer(d):
        return lax.rem(me + d, n)

    barrier = pltpu.get_barrier_semaphore()
    for d in range(1, n):
        pl.semaphore_signal(barrier, inc=1, device_id=(peer(d), col), device_id_type=MESH)
    for c in (left, right):
        pl.semaphore_signal(barrier, inc=1, device_id=(me, c), device_id_type=MESH)

    def send(src, dst, ss, rs, device):
        copy = pltpu.make_async_remote_copy(
            src_ref=src, dst_ref=dst, send_sem=ss, recv_sem=rs,
            device_id=device, device_id_type=MESH,
        )
        copy.start()
        return copy

    loads = [
        pltpu.make_async_copy(src, dst, in_sem.at[i])
        for i, (src, dst) in enumerate((
            (bg_hbm, bg_ref), (idx_hbm, idx_ref), (yobs_hbm, yobs_ref),
            (list_hbm, list_ref), (count_hbm, count_ref), (weight_hbm, weight_ref),
        ))
    ]
    for load in loads:
        load.start()

    for load in loads[:3]:
        load.wait()
    tail = (m // 16) * 16
    for q in range(n):
        bgp[q, tail:pad, :] = jnp.zeros((pad - tail, cells), BF16)
        bgp[q, 0:m, :] = bg_ref[:, q * cells:(q + 1) * cells]

    yloc[...] = jnp.broadcast_to(yobs_ref[...].astype(F32), yloc.shape)
    ybuf[1] = yloc[...]


    pl.semaphore_wait(barrier, n + 1)

    y_up = send(yloc, ybuf.at[0], y_ss.at[0], y_rs.at[0], (peer(1), col))
    y_down = send(yloc, ybuf.at[2], y_ss.at[1], y_rs.at[1], (peer(n - 1), col))

    def observe(row):
        hot = lax.broadcasted_iota(jnp.int32, (cells, width), 0) == idx_ref[pl.ds(row, 1), :]
        hot = jnp.where(hot, 1.0, 0.0).astype(BF16)
        return jnp.dot(bgp[row], hot, preferred_element_type=F32).astype(BF16)

    obs_copies = []
    if n == 4:
        side = me // 2

        def turn(x, last):
            return x + side * (last - 2 * x)

        here = turn(me, 3)
        inner = here == 1
        other = 1 - here

        def obs_send(row, dest, slot, i):
            return send(
                obs_loc.at[row], obuf.at[me, turn(slot, 2)], obs_ss.at[i],
                obs_rs.at[me, turn(slot, 2)], (turn(dest, 3), col),
            )

        def landed(source, slot):
            return pltpu.make_async_remote_copy(
                src_ref=obs_loc.at[0], dst_ref=obuf.at[turn(source, 3), turn(slot, 2)],
                send_sem=obs_ss.at[0], recv_sem=obs_rs.at[turn(source, 3), turn(slot, 2)],
                device_id=(turn(other, 3), col), device_id_type=MESH,
            )

        for i, (row, dest, slot) in enumerate(((2, 2, 1), (3, 2, 2), (1, 2, 0), (0, 3, 2))):
            obs_loc[row] = observe(turn(row, 3))
            obs_copies.append(obs_send(row, dest, slot, i))
        def kth(place, k):
            return (2 - place, 1 - place, 2 * place)[k]

        for k in range(3):
            slot = kth(other, k)
            obs_copies.append(obs_send(lax.rem(other + slot + 3, 4), other, slot, 4 + k))
        for slot in range(3):
            obuf[me, turn(slot, 2)] = obs_loc[lax.rem(here + slot + 3, 4)]

        handed = ((2, 1), (2, 0), (3, 1), (3, 0))

        def hand_on(i, source, slot):
            return pltpu.make_async_remote_copy(
                src_ref=obuf.at[turn(source, 3), turn(slot, 2)],
                dst_ref=obuf.at[turn(source, 3), turn(slot + 1, 2)],
                send_sem=obs_ss.at[7 + i], recv_sem=obs_rs.at[turn(source, 3), turn(slot + 1, 2)],
                device_id=(turn(0, 3), col), device_id_type=MESH,
            )
    else:
        for t in sorted(range(n), key=lambda t: -min(t, n - t)):
            obs_loc[t] = observe(peer(t))
            for slot in (0, 1, 2):
                d = (t + 1 - slot) % n
                if d == 0:
                    obuf[me, slot] = obs_loc[t]
                else:
                    obs_copies.append(
                        send(
                            obs_loc.at[t], obuf.at[me, slot], obs_ss.at[3 * d + slot],
                            obs_rs.at[d, slot], (peer(d), col),
                        )
                    )

    for load in loads[3:]:
        load.wait()
    length = list_ref.shape[1]
    place = lax.broadcasted_iota(jnp.int32, (1, length), 1)
    live = jnp.where(place < count_ref[...], weight_ref[...], 0.0)
    part0 = live.astype(BF16)
    rest = live - part0.astype(F32)
    part1 = rest.astype(BF16)
    part2 = (rest - part1.astype(F32)).astype(BF16)
    cand = list_ref[...]
    strip = cand // lanes
    lane = cand - strip * lanes
    group = strip // (3 * strips)
    strip = strip + group * (block - 3 * strips)
    rows_at = lax.broadcasted_iota(jnp.int32, (3 * block, length), 0) == strip
    lanes_at = lax.broadcasted_iota(jnp.int32, (lanes, length), 0) == lane
    lane_hot = jnp.where(lanes_at, 1.0, 0.0).astype(BF16)
    spread = [
        dot_t(jnp.where(rows_at, part.astype(F32), 0.0).astype(BF16), lane_hot)
        for part in (part0, part1, part2)
    ]
    wd[...] = spread[0] + (spread[1] + spread[2])
    w_left = send(wd.at[pl.ds(0, block)], wbuf.at[0], w_ss.at[0], w_rs.at[0], (me, left))
    w_right = send(wd.at[pl.ds(2 * block, block)], wbuf.at[1], w_ss.at[1], w_rs.at[1], (me, right))

    if n == 4:
        @pl.when(inner)
        def _():
            for i, (source, slot) in enumerate(handed):
                landed(source, slot).wait_recv()
                hand_on(i, source, slot).start()

    def take(k):
        if n != 4:
            if k == 0:
                for copy in obs_copies:
                    copy.wait_recv()
            return k
        slot = kth(here, k)
        if k == 2:
            for source in (2, 3):
                landed(source, slot).wait_recv()
        else:
            @pl.when(jnp.logical_not(inner))
            def _():
                for source in (2, 3):
                    landed(source, slot).wait_recv()
        landed(other, slot).wait_recv()
        return turn(slot, 2)

    row_id = lax.broadcasted_iota(jnp.int32, (total, 1), 0)
    real = lax.rem(row_id, pad) < m

    def perturbed(slot):
        seen = obuf[:, slot].reshape(total, width).astype(F32)
        mean = jnp.sum(seen, axis=0, keepdims=True) / members
        innov = ybuf[slot][0:1, :] - mean
        values = jnp.where(real, seen - mean, jnp.where(row_id == m, innov, 0.0))
        return values.astype(BF16)

    def term(values, weights, slot):
        strip_rows = [weights[pl.ds(slot * strips + i, 1), :] for i in range(strips)]
        scale = jnp.concatenate(strip_rows, axis=1)
        return dot_t((values.astype(F32) * scale).astype(BF16), values)

    tables = (wbuf.at[0], wbuf.at[1], wd.at[pl.ds(block, block)])
    for k in range(2):
        slot = take(k)
        if k == 0:
            for copy in (y_up, y_down, w_left, w_right):
                copy.wait_recv()
        values = perturbed(slot)
        for i, table in enumerate(tables):
            if k == 0:
                gacc[i] = term(values, table, slot)
            else:
                gacc[i] += term(values, table, slot)
    slot = take(2)

    state_copies = []
    for d in range(n - 1, 0, -1):
        state_copies.append(
            send(bgp.at[peer(d)], sbuf.at[me], st_ss.at[d], st_rs.at[d], (peer(d), col))
        )
    sbuf[me] = bgp[me]

    values = perturbed(slot)
    gsend[0] = (gacc[0] + term(values, tables[0], slot)).astype(BF16)
    g_right = send(gsend.at[0], grecv.at[0], g_ss.at[0], g_rs.at[0], (me, right))
    gsend[1] = (gacc[1] + term(values, tables[1], slot)).astype(BF16)
    g_left = send(gsend.at[1], grecv.at[1], g_ss.at[1], g_rs.at[1], (me, left))
    own = gacc[2] + term(values, tables[2], slot)
    g_right.wait_recv()
    g_left.wait_recv()
    full = own + (grecv[0].astype(F32) + grecv[1].astype(F32))

    col_id = lax.broadcasted_iota(jnp.int32, (1, total), 1)
    real_col = lax.rem(col_id, pad) < m
    same = row_id == col_id
    eye = jnp.where(same, 1.0, 0.0)
    drive = jnp.where(real_col, full[m:m + 1, :], 0.0)
    gram = jnp.where(real & real_col, full, 0.0)
    gram = gram + jnp.where(same & real, (members - 1) / INFLATION, 0.0)
    norm = jnp.sqrt(jnp.sum(jnp.sum(gram * gram, axis=0, keepdims=True), axis=1, keepdims=True))
    root = newton(gram, norm, eye, NS_STEPS)
    product = jnp.sum(root * drive, axis=1, keepdims=True)
    shift = jnp.sum(root * product, axis=0, keepdims=True)
    wt[...] = (math.sqrt(members - 1) / jnp.sqrt(norm) * root + shift / norm).astype(BF16)

    for copy in state_copies:
        copy.wait_recv()
    states = sbuf[...].reshape(total, cells).astype(F32)
    state_mean = jnp.sum(states, axis=0, keepdims=True) / members
    state_pert = jnp.where(real, states - state_mean, 0.0).astype(BF16)

    mine = pl.ds(pl.multiple_of(me * cells, 128), cells)
    out_copies = []
    for d in list(range(n - 1, 0, -1)) + [0]:
        dest = peer(d)
        rows = wt[pl.ds(pl.multiple_of(dest * pad, 16), pad), :]
        result = (state_mean + jnp.dot(rows, state_pert, preferred_element_type=F32)).astype(BF16)
        if d == 0:
            out_ref[:, mine] = result
        else:
            oloc[d] = result
            out_copies.append(
                send(oloc.at[d], out_ref.at[:, mine], o_ss.at[d], o_rs.at[d], (dest, col))
            )
    for copy in out_copies:
        copy.wait_recv()
    for copy in obs_copies + state_copies + out_copies:
        copy.wait_send()
    for copy in (w_left, w_right, y_up, y_down, g_right, g_left):
        copy.wait_send()
    if n == 4:
        @pl.when(inner)
        def _():
            for i, (source, slot) in enumerate(handed):
                hand_on(i, source, slot).wait_send()


def local(background, obs_index, yobs, loc_list, loc_count, loc_weight):
    n, regs = lax.axis_size("mem"), lax.axis_size("reg")
    m = background.shape[0]
    rows, width = obs_index.shape[1], obs_index.shape[2]
    cells = background.shape[2] // rows
    length = loc_list.shape[2]
    pad = (m // 16 + 1) * 16
    total = n * pad
    block = -(-3 * (width // 128) // 8) * 8
    vmem = pl.BlockSpec(memory_space=pltpu.VMEM)
    dma = pltpu.SemaphoreType.DMA
    result = pl.pallas_call(
        functools.partial(kernel, n, regs, m, pad, width, cells),
        out_shape=jax.ShapeDtypeStruct((pad, rows * cells), BF16),
        in_specs=[pl.BlockSpec(memory_space=pltpu.HBM)] * 6,
        out_specs=vmem,
        scratch_shapes=[
            pltpu.VMEM((m, rows * cells), BF16),
            pltpu.VMEM((rows, width), jnp.int32),
            pltpu.VMEM((1, width), BF16),
            pltpu.VMEM((1, length), jnp.int32),
            pltpu.VMEM((1, 1), jnp.int32),
            pltpu.VMEM((1, length), F32),
            pltpu.VMEM((n, pad, cells), BF16),
            pltpu.VMEM((n, pad, width), BF16),
            pltpu.VMEM((n, 3, pad, width), BF16),
            pltpu.VMEM((n, pad, cells), BF16),
            pltpu.VMEM((3 * block, 128), F32),
            pltpu.VMEM((2, block, 128), F32),
            pltpu.VMEM((8, width), F32),
            pltpu.VMEM((3, 8, width), F32),
            pltpu.VMEM((3, total, total), F32),
            pltpu.VMEM((2, total, total), BF16),
            pltpu.VMEM((2, total, total), BF16),
            pltpu.VMEM((total, total), BF16),
            pltpu.VMEM((n, pad, cells), BF16),
            dma((3 * n,)), dma((n, 3)),
            dma((n,)), dma((n,)),
            dma((2,)), dma((2,)),
            dma((2,)), dma((2,)),
            dma((2,)), dma((2,)),
            dma((n,)), dma((n,)), dma((6,)),
        ],
        compiler_params=pltpu.CompilerParams(
            collective_id=0, has_side_effects=True
        ),
    )(
        background.reshape(m, rows * cells),
        obs_index.reshape(rows, width),
        yobs.reshape(1, width),
        loc_list.reshape(1, length),
        loc_count.reshape(1, 1),
        loc_weight.reshape(1, length),
    )
    return result[:m].reshape(m, 1, rows * cells)


def solution(mesh):
    return jax.shard_map(
        local,
        mesh=mesh,
        in_specs=(
            P("mem", "reg", None),
            P("reg", None, None),
            P("reg", "mem", None),
            P("reg", "mem", None),
            P("reg", "mem"),
            P("reg", "mem", None),
        ),
        out_specs=P("mem", "reg", None),
        check_vma=False,
    )
```

```python
import functools
import math

import jax
import jax.numpy as jnp
from jax import lax
from jax.experimental import pallas as pl
from jax.experimental.pallas import tpu as pltpu
from jax.sharding import PartitionSpec as P

NS_STEPS = 5
INFLATION = 1.1
MESH = pl.DeviceIdType.MESH
F32 = jnp.float32
BF16 = jnp.bfloat16


def split(x):
    high = x.astype(BF16)
    return high, (x - high.astype(F32)).astype(BF16)


def mm(a, b):
    return (
        jnp.dot(a[0], b[1], preferred_element_type=F32)
        + jnp.dot(a[1], b[0], preferred_element_type=F32)
        + jnp.dot(a[0], b[0], preferred_element_type=F32)
    )


def dot_t(a, b):
    return lax.dot_general(a, b, (((1,), (1,)), ((), ())), preferred_element_type=F32)


def newton(gram, norm, eye, steps):
    current = gram * (1.0 / norm)
    root = None
    for step in range(steps):
        last = step == steps - 1
        if root is None:
            corr = 1.5 * eye - 0.5 * current
            corr_s = split(corr)
            root = corr
        else:
            cur_s, root_s = split(current), split(root)
            corr = 1.5 * eye - 0.5 * mm(root_s, cur_s)
            corr_s = split(corr)
            root = mm(corr_s, root_s)
        if not last:
            current = mm(split(current), corr_s)
    return root


def kernel(
    n, regs, m, pad, width, cells,
    bg_hbm, idx_hbm, yobs_hbm, list_hbm, count_hbm, weight_hbm,
    out_ref,
    bg_ref, idx_ref, yobs_ref, list_ref, count_ref, weight_ref,
    bgp, obs_loc, obuf, sbuf, wd, wbuf, yloc, ybuf, gacc, gsend, grecv, wt, oloc, oland,
    obs_ss, obs_rs, st_ss, st_rs, w_ss, w_rs, y_ss, y_rs, g_ss, g_rs, o_ss, o_rs, in_sem,
):
    me, col = lax.axis_index("mem"), lax.axis_index("reg")
    left, right = lax.rem(col + regs - 1, regs), lax.rem(col + 1, regs)
    members, total = n * m, n * pad
    lanes = 128
    strips = width // lanes
    block = wd.shape[0] // 3

    def peer(d):
        return lax.rem(me + d, n)

    barrier = pltpu.get_barrier_semaphore()
    for d in range(1, n):
        pl.semaphore_signal(barrier, inc=1, device_id=(peer(d), col), device_id_type=MESH)
    for c in (left, right):
        pl.semaphore_signal(barrier, inc=1, device_id=(me, c), device_id_type=MESH)

    def send(src, dst, ss, rs, device):
        copy = pltpu.make_async_remote_copy(
            src_ref=src, dst_ref=dst, send_sem=ss, recv_sem=rs,
            device_id=device, device_id_type=MESH,
        )
        copy.start()
        return copy

    loads = [
        pltpu.make_async_copy(src, dst, in_sem.at[i])
        for i, (src, dst) in enumerate((
            (bg_hbm, bg_ref), (idx_hbm, idx_ref), (yobs_hbm, yobs_ref),
            (list_hbm, list_ref), (count_hbm, count_ref), (weight_hbm, weight_ref),
        ))
    ]
    for load in loads:
        load.start()

    for load in loads[:3]:
        load.wait()
    tail = (m // 16) * 16
    for q in range(n):
        bgp[q, tail:pad, :] = jnp.zeros((pad - tail, cells), BF16)
        bgp[q, 0:m, :] = bg_ref[:, q * cells:(q + 1) * cells]

    yloc[...] = jnp.broadcast_to(yobs_ref[...].astype(F32), yloc.shape)
    ybuf[1] = yloc[...]

    pl.semaphore_wait(barrier, n + 1)

    y_up = send(yloc, ybuf.at[0], y_ss.at[0], y_rs.at[0], (peer(1), col))
    y_down = send(yloc, ybuf.at[2], y_ss.at[1], y_rs.at[1], (peer(n - 1), col))

    def observe(row):
        hot = lax.broadcasted_iota(jnp.int32, (cells, width), 0) == idx_ref[pl.ds(row, 1), :]
        hot = jnp.where(hot, 1.0, 0.0).astype(BF16)
        return jnp.dot(bgp[row], hot, preferred_element_type=F32).astype(BF16)

    obs_copies = []
    if n == 4:
        side = me // 2

        def turn(x, last):
            return x + side * (last - 2 * x)

        here = turn(me, 3)
        inner = here == 1
        other = 1 - here

        def obs_send(row, dest, slot, i):
            return send(
                obs_loc.at[row], obuf.at[me, turn(slot, 2)], obs_ss.at[i],
                obs_rs.at[me, turn(slot, 2)], (turn(dest, 3), col),
            )

        def landed(source, slot):
            return pltpu.make_async_remote_copy(
                src_ref=obs_loc.at[0], dst_ref=obuf.at[turn(source, 3), turn(slot, 2)],
                send_sem=obs_ss.at[0], recv_sem=obs_rs.at[turn(source, 3), turn(slot, 2)],
                device_id=(turn(other, 3), col), device_id_type=MESH,
            )

        for i, (row, dest, slot) in enumerate(((2, 2, 1), (3, 2, 2), (1, 2, 0), (0, 3, 2))):
            obs_loc[row] = observe(turn(row, 3))
            obs_copies.append(obs_send(row, dest, slot, i))
        def kth(place, k):
            return (2 - place, 1 - place, 2 * place)[k]

        for k in range(3):
            slot = kth(other, k)
            obs_copies.append(obs_send(lax.rem(other + slot + 3, 4), other, slot, 4 + k))
        for slot in range(3):
            obuf[me, turn(slot, 2)] = obs_loc[lax.rem(here + slot + 3, 4)]

        handed = ((2, 1), (2, 0), (3, 1), (3, 0))

        def hand_on(i, source, slot):
            return pltpu.make_async_remote_copy(
                src_ref=obuf.at[turn(source, 3), turn(slot, 2)],
                dst_ref=obuf.at[turn(source, 3), turn(slot + 1, 2)],
                send_sem=obs_ss.at[7 + i], recv_sem=obs_rs.at[turn(source, 3), turn(slot + 1, 2)],
                device_id=(turn(0, 3), col), device_id_type=MESH,
            )
    else:
        for t in sorted(range(n), key=lambda t: -min(t, n - t)):
            obs_loc[t] = observe(peer(t))
            for slot in (0, 1, 2):
                d = (t + 1 - slot) % n
                if d == 0:
                    obuf[me, slot] = obs_loc[t]
                else:
                    obs_copies.append(
                        send(
                            obs_loc.at[t], obuf.at[me, slot], obs_ss.at[3 * d + slot],
                            obs_rs.at[d, slot], (peer(d), col),
                        )
                    )

    for load in loads[3:]:
        load.wait()
    length = list_ref.shape[1]
    place = lax.broadcasted_iota(jnp.int32, (1, length), 1)
    live = jnp.where(place < count_ref[...], weight_ref[...], 0.0)
    part0 = live.astype(BF16)
    rest = live - part0.astype(F32)
    part1 = rest.astype(BF16)
    part2 = (rest - part1.astype(F32)).astype(BF16)
    cand = list_ref[...]
    strip = cand // lanes
    lane = cand - strip * lanes
    group = strip // (3 * strips)
    strip = strip + group * (block - 3 * strips)
    rows_at = lax.broadcasted_iota(jnp.int32, (3 * block, length), 0) == strip
    lanes_at = lax.broadcasted_iota(jnp.int32, (lanes, length), 0) == lane
    lane_hot = jnp.where(lanes_at, 1.0, 0.0).astype(BF16)
    spread = [
        dot_t(jnp.where(rows_at, part.astype(F32), 0.0).astype(BF16), lane_hot)
        for part in (part0, part1, part2)
    ]
    wd[...] = spread[0] + (spread[1] + spread[2])
    w_left = send(wd.at[pl.ds(0, block)], wbuf.at[0], w_ss.at[0], w_rs.at[0], (me, left))
    w_right = send(wd.at[pl.ds(2 * block, block)], wbuf.at[1], w_ss.at[1], w_rs.at[1], (me, right))

    def state_send(dest, i):
        return send(bgp.at[dest], sbuf.at[me], st_ss.at[i], st_rs.at[me], (dest, col))

    sbuf[me] = bgp[me]
    if n == 4:
        state_copies = [state_send(turn(2, 3), 0)]
        state_later = [turn(3, 3), turn(other, 3)]
    else:
        state_copies = []
        state_later = [peer(d) for d in range(n - 1, 0, -1)]

    if n == 4:
        @pl.when(inner)
        def _():
            for i, (source, slot) in enumerate(handed):
                landed(source, slot).wait_recv()
                hand_on(i, source, slot).start()

    def take(k):
        if n != 4:
            if k == 0:
                for copy in obs_copies:
                    copy.wait_recv()
            return k
        slot = kth(here, k)
        if k == 2:
            for source in (2, 3):
                landed(source, slot).wait_recv()
        else:
            @pl.when(jnp.logical_not(inner))
            def _():
                for source in (2, 3):
                    landed(source, slot).wait_recv()
        landed(other, slot).wait_recv()
        return turn(slot, 2)

    row_id = lax.broadcasted_iota(jnp.int32, (total, 1), 0)
    real = lax.rem(row_id, pad) < m

    def perturbed(slot):
        seen = obuf[:, slot].reshape(total, width).astype(F32)
        mean = jnp.sum(seen, axis=0, keepdims=True) / members
        innov = ybuf[slot][0:1, :] - mean
        values = jnp.where(real, seen - mean, jnp.where(row_id == m, innov, 0.0))
        return values.astype(BF16)

    def term(values, weights, slot):
        strip_rows = [weights[pl.ds(slot * strips + i, 1), :] for i in range(strips)]
        scale = jnp.concatenate(strip_rows, axis=1)
        return dot_t((values.astype(F32) * scale).astype(BF16), values)

    tables = (wbuf.at[0], wbuf.at[1], wd.at[pl.ds(block, block)])
    for k in range(2):
        slot = take(k)
        if k == 0:
            for copy in (y_up, y_down, w_left, w_right):
                copy.wait_recv()
        values = perturbed(slot)
        for i, table in enumerate(tables):
            if k == 0:
                gacc[i] = term(values, table, slot)
            else:
                gacc[i] += term(values, table, slot)
        if k == 0:
            for dest in state_later:
                state_copies.append(state_send(dest, len(state_copies)))
    slot = take(2)

    values = perturbed(slot)
    gsend[0] = (gacc[0] + term(values, tables[0], slot)).astype(BF16)
    g_right = send(gsend.at[0], grecv.at[0], g_ss.at[0], g_rs.at[0], (me, right))
    gsend[1] = (gacc[1] + term(values, tables[1], slot)).astype(BF16)
    g_left = send(gsend.at[1], grecv.at[1], g_ss.at[1], g_rs.at[1], (me, left))
    own = gacc[2] + term(values, tables[2], slot)
    g_right.wait_recv()
    g_left.wait_recv()
    full = own + (grecv[0].astype(F32) + grecv[1].astype(F32))

    col_id = lax.broadcasted_iota(jnp.int32, (1, total), 1)
    real_col = lax.rem(col_id, pad) < m
    same = row_id == col_id
    eye = jnp.where(same, 1.0, 0.0)
    drive = jnp.where(real_col, full[m:m + 1, :], 0.0)
    gram = jnp.where(real & real_col, full, 0.0)
    gram = gram + jnp.where(same & real, (members - 1) / INFLATION, 0.0)
    norm = jnp.sqrt(jnp.sum(jnp.sum(gram * gram, axis=0, keepdims=True), axis=1, keepdims=True))
    root = newton(gram, norm, eye, NS_STEPS)
    product = jnp.sum(root * drive, axis=1, keepdims=True)
    shift = jnp.sum(root * product, axis=0, keepdims=True)
    wt[...] = (math.sqrt(members - 1) / jnp.sqrt(norm) * root + shift / norm).astype(BF16)

    for d in range(1, n):
        pltpu.make_async_remote_copy(
            src_ref=bgp.at[0], dst_ref=sbuf.at[peer(d)], send_sem=st_ss.at[0], recv_sem=st_rs.at[peer(d)],
            device_id=(peer(d), col), device_id_type=MESH,
        ).wait_recv()
    states = sbuf[...].reshape(total, cells).astype(F32)
    state_mean = jnp.sum(states, axis=0, keepdims=True) / members
    state_pert = jnp.where(real, states - state_mean, 0.0).astype(BF16)

    out_copies = []
    for d in list(range(n - 1, 0, -1)) + [0]:
        dest = peer(d)
        rows = wt[pl.ds(pl.multiple_of(dest * pad, 16), pad), :]
        result = (state_mean + jnp.dot(rows, state_pert, preferred_element_type=F32)).astype(BF16)
        if d == 0:
            oland[me] = result
        else:
            oloc[d] = result
            out_copies.append(
                send(oloc.at[d], oland.at[me], o_ss.at[d], o_rs.at[d], (dest, col))
            )

    def finish(source):
        out_ref[:, pl.ds(pl.multiple_of(source * cells, 128), cells)] = oland[source, 0:m, :]

    finish(me)
    for d, copy in reversed(list(zip(range(n - 1, 0, -1), out_copies))):
        copy.wait_recv()
        finish(peer(n - d))
    for copy in obs_copies + state_copies + out_copies:
        copy.wait_send()
    for copy in (w_left, w_right, y_up, y_down, g_right, g_left):
        copy.wait_send()
    if n == 4:
        @pl.when(inner)
        def _():
            for i, (source, slot) in enumerate(handed):
                hand_on(i, source, slot).wait_send()


def local(background, obs_index, yobs, loc_list, loc_count, loc_weight):
    n, regs = lax.axis_size("mem"), lax.axis_size("reg")
    m = background.shape[0]
    rows, width = obs_index.shape[1], obs_index.shape[2]
    cells = background.shape[2] // rows
    length = loc_list.shape[2]
    pad = (m // 16 + 1) * 16
    total = n * pad
    block = -(-3 * (width // 128) // 8) * 8
    vmem = pl.BlockSpec(memory_space=pltpu.VMEM)
    dma = pltpu.SemaphoreType.DMA
    result = pl.pallas_call(
        functools.partial(kernel, n, regs, m, pad, width, cells),
        out_shape=jax.ShapeDtypeStruct((m, rows * cells), BF16),
        in_specs=[pl.BlockSpec(memory_space=pltpu.HBM)] * 6,
        out_specs=vmem,
        scratch_shapes=[
            pltpu.VMEM((m, rows * cells), BF16),
            pltpu.VMEM((rows, width), jnp.int32),
            pltpu.VMEM((1, width), BF16),
            pltpu.VMEM((1, length), jnp.int32),
            pltpu.VMEM((1, 1), jnp.int32),
            pltpu.VMEM((1, length), F32),
            pltpu.VMEM((n, pad, cells), BF16),
            pltpu.VMEM((n, pad, width), BF16),
            pltpu.VMEM((n, 3, pad, width), BF16),
            pltpu.VMEM((n, pad, cells), BF16),
            pltpu.VMEM((3 * block, 128), F32),
            pltpu.VMEM((2, block, 128), F32),
            pltpu.VMEM((8, width), F32),
            pltpu.VMEM((3, 8, width), F32),
            pltpu.VMEM((3, total, total), F32),
            pltpu.VMEM((2, total, total), BF16),
            pltpu.VMEM((2, total, total), BF16),
            pltpu.VMEM((total, total), BF16),
            pltpu.VMEM((n, pad, cells), BF16),
            pltpu.VMEM((n, pad, cells), BF16),
            dma((3 * n,)), dma((n, 3)),
            dma((n,)), dma((n,)),
            dma((2,)), dma((2,)),
            dma((2,)), dma((2,)),
            dma((2,)), dma((2,)),
            dma((n,)), dma((n,)), dma((6,)),
        ],
        compiler_params=pltpu.CompilerParams(
            collective_id=0, has_side_effects=True
        ),
    )(
        background.reshape(m, rows * cells),
        obs_index.reshape(rows, width),
        yobs.reshape(1, width),
        loc_list.reshape(1, length),
        loc_count.reshape(1, 1),
        loc_weight.reshape(1, length),
    )
    return result.reshape(m, 1, rows * cells)


def solution(mesh):
    return jax.shard_map(
        local,
        mesh=mesh,
        in_specs=(
            P("mem", "reg", None),
            P("reg", None, None),
            P("reg", "mem", None),
            P("reg", "mem", None),
            P("reg", "mem"),
            P("reg", "mem", None),
        ),
        out_specs=P("mem", "reg", None),
        check_vma=False,
    )
```

```python
import functools
import math

import jax
import jax.numpy as jnp
from jax import lax
from jax.experimental import pallas as pl
from jax.experimental.pallas import tpu as pltpu
from jax.sharding import PartitionSpec as P

NS_STEPS = 5
INFLATION = 1.1
MESH = pl.DeviceIdType.MESH
F32 = jnp.float32
BF16 = jnp.bfloat16


def split(x):
    high = x.astype(BF16)
    return high, (x - high.astype(F32)).astype(BF16)


def mm(a, b, passes):
    top = jnp.dot(a[0], b[0], preferred_element_type=F32)
    if passes == 1:
        return top
    return (
        jnp.dot(a[0], b[1], preferred_element_type=F32)
        + jnp.dot(a[1], b[0], preferred_element_type=F32)
        + top
    )


def dot_t(a, b):
    return lax.dot_general(a, b, (((1,), (1,)), ((), ())), preferred_element_type=F32)


def newton(gram, norm, eye, steps):
    t = gram * (1.0 / norm)
    root = None
    for step in range(steps):
        passes = 1 if step < steps - 2 else 3
        t_s = split(t)
        if root is None:
            root = 1.5 * eye - 0.5 * t
        else:
            root = 1.5 * root - 0.5 * mm(t_s, split(root), passes)
        if step < steps - 1:
            square = mm(t_s, t_s, passes)
            t = 2.25 * t - 1.5 * square + 0.25 * mm(t_s, split(square), passes)
    return root


def kernel(
    n, regs, m, pad, width, cells,
    bg_hbm, idx_hbm, yobs_hbm, list_hbm, weight_hbm, count_ref,
    out_ref,
    bg_ref, idx_ref, yobs_ref, list_ref, weight_ref,
    bgp, obs_loc, obuf, sbuf, wd, wbuf, yloc, ybuf, gacc, gsend, grecv, wt, oloc, oland,
    obs_ss, obs_rs, st_ss, st_rs, w_ss, w_rs, y_ss, y_rs, g_ss, g_rs, o_ss, o_rs, in_sem,
):
    me, col = lax.axis_index("mem"), lax.axis_index("reg")
    left, right = lax.rem(col + regs - 1, regs), lax.rem(col + 1, regs)
    members, total = n * m, n * pad
    lanes = 128
    strips = width // lanes
    block = wd.shape[0] // 3

    def peer(d):
        return lax.rem(me + d, n)

    barrier = pltpu.get_barrier_semaphore()
    for d in range(1, n):
        pl.semaphore_signal(barrier, inc=1, device_id=(peer(d), col), device_id_type=MESH)
    for c in (left, right):
        pl.semaphore_signal(barrier, inc=1, device_id=(me, c), device_id_type=MESH)

    def send(src, dst, ss, rs, device):
        copy = pltpu.make_async_remote_copy(
            src_ref=src, dst_ref=dst, send_sem=ss, recv_sem=rs,
            device_id=device, device_id_type=MESH,
        )
        copy.start()
        return copy

    loads = [
        pltpu.make_async_copy(src, dst, in_sem.at[i])
        for i, (src, dst) in enumerate((
            (bg_hbm, bg_ref), (idx_hbm, idx_ref), (yobs_hbm, yobs_ref),
            (list_hbm, list_ref), (weight_hbm, weight_ref),
        ))
    ]
    for load in loads:
        load.start()

    for load in loads[:3]:
        load.wait()
    tail = (m // 16) * 16
    for q in range(n):
        bgp[q, tail:pad, :] = jnp.zeros((pad - tail, cells), BF16)
        bgp[q, 0:m, :] = bg_ref[:, q * cells:(q + 1) * cells]

    yloc[...] = jnp.broadcast_to(yobs_ref[...].astype(F32), yloc.shape)
    ybuf[1] = yloc[...]

    pl.semaphore_wait(barrier, n + 1)

    y_up = send(yloc, ybuf.at[0], y_ss.at[0], y_rs.at[0], (peer(1), col))
    y_down = send(yloc, ybuf.at[2], y_ss.at[1], y_rs.at[1], (peer(n - 1), col))

    def observe(row):
        hot = lax.broadcasted_iota(jnp.int32, (cells, width), 0) == idx_ref[pl.ds(row, 1), :]
        hot = jnp.where(hot, 1.0, 0.0).astype(BF16)
        return jnp.dot(bgp[row], hot, preferred_element_type=F32).astype(BF16)

    obs_copies = []
    if n == 4:
        side = me // 2

        def turn(x, last):
            return x + side * (last - 2 * x)

        here = turn(me, 3)
        inner = here == 1
        other = 1 - here

        def obs_send(row, dest, slot, i):
            return send(
                obs_loc.at[row], obuf.at[me, turn(slot, 2)], obs_ss.at[i],
                obs_rs.at[me, turn(slot, 2)], (turn(dest, 3), col),
            )

        def landed(source, slot):
            return pltpu.make_async_remote_copy(
                src_ref=obs_loc.at[0], dst_ref=obuf.at[turn(source, 3), turn(slot, 2)],
                send_sem=obs_ss.at[0], recv_sem=obs_rs.at[turn(source, 3), turn(slot, 2)],
                device_id=(turn(other, 3), col), device_id_type=MESH,
            )

        for i, (row, dest, slot) in enumerate(((2, 2, 1), (3, 2, 2), (1, 2, 0), (0, 3, 2))):
            obs_loc[row] = observe(turn(row, 3))
            obs_copies.append(obs_send(row, dest, slot, i))
        def kth(place, k):
            return (2 - place, 1 - place, 2 * place)[k]

        for k in range(3):
            slot = kth(other, k)
            obs_copies.append(obs_send(lax.rem(other + slot + 3, 4), other, slot, 4 + k))
        for slot in range(3):
            obuf[me, turn(slot, 2)] = obs_loc[lax.rem(here + slot + 3, 4)]

        handed = ((2, 1), (2, 0), (3, 1), (3, 0))

        def hand_on(i, source, slot):
            return pltpu.make_async_remote_copy(
                src_ref=obuf.at[turn(source, 3), turn(slot, 2)],
                dst_ref=obuf.at[turn(source, 3), turn(slot + 1, 2)],
                send_sem=obs_ss.at[7 + i], recv_sem=obs_rs.at[turn(source, 3), turn(slot + 1, 2)],
                device_id=(turn(0, 3), col), device_id_type=MESH,
            )
    else:
        for t in sorted(range(n), key=lambda t: -min(t, n - t)):
            obs_loc[t] = observe(peer(t))
            for slot in (0, 1, 2):
                d = (t + 1 - slot) % n
                if d == 0:
                    obuf[me, slot] = obs_loc[t]
                else:
                    obs_copies.append(
                        send(
                            obs_loc.at[t], obuf.at[me, slot], obs_ss.at[3 * d + slot],
                            obs_rs.at[d, slot], (peer(d), col),
                        )
                    )

    for load in loads[3:]:
        load.wait()
    length = list_ref.shape[1]
    place = lax.broadcasted_iota(jnp.int32, (1, length), 1)
    live = jnp.where(place < count_ref[0, 0], weight_ref[...], 0.0)
    part0 = live.astype(BF16)
    rest = live - part0.astype(F32)
    part1 = rest.astype(BF16)
    part2 = (rest - part1.astype(F32)).astype(BF16)
    cand = list_ref[...]
    strip = cand // lanes
    lane = cand - strip * lanes
    group = strip // (3 * strips)
    strip = strip + group * (block - 3 * strips)
    rows_at = lax.broadcasted_iota(jnp.int32, (3 * block, length), 0) == strip
    lanes_at = lax.broadcasted_iota(jnp.int32, (lanes, length), 0) == lane
    lane_hot = jnp.where(lanes_at, 1.0, 0.0).astype(BF16)
    spread = [
        dot_t(jnp.where(rows_at, part.astype(F32), 0.0).astype(BF16), lane_hot)
        for part in (part0, part1, part2)
    ]
    wd[...] = spread[0] + (spread[1] + spread[2])
    w_left = send(wd.at[pl.ds(0, block)], wbuf.at[0], w_ss.at[0], w_rs.at[0], (me, left))
    w_right = send(wd.at[pl.ds(2 * block, block)], wbuf.at[1], w_ss.at[1], w_rs.at[1], (me, right))

    def state_send(dest, i):
        return send(bgp.at[dest], sbuf.at[me], st_ss.at[i], st_rs.at[me], (dest, col))

    sbuf[me] = bgp[me]
    if n == 4:
        state_copies = [state_send(turn(2, 3), 0)]
        state_later = [turn(3, 3), turn(other, 3)]
    else:
        state_copies = []
        state_later = [peer(d) for d in range(n - 1, 0, -1)]

    if n == 4:
        @pl.when(inner)
        def _():
            for i, (source, slot) in enumerate(handed):
                landed(source, slot).wait_recv()
                hand_on(i, source, slot).start()

    def take(k):
        if n != 4:
            if k == 0:
                for copy in obs_copies:
                    copy.wait_recv()
            return k
        slot = kth(here, k)
        if k == 2:
            for source in (2, 3):
                landed(source, slot).wait_recv()
        else:
            @pl.when(jnp.logical_not(inner))
            def _():
                for source in (2, 3):
                    landed(source, slot).wait_recv()
        landed(other, slot).wait_recv()
        return turn(slot, 2)

    row_id = lax.broadcasted_iota(jnp.int32, (total, 1), 0)
    real = lax.rem(row_id, pad) < m

    def perturbed(slot):
        seen = obuf[:, slot].reshape(total, width).astype(F32)
        mean = jnp.sum(seen, axis=0, keepdims=True) / members
        innov = ybuf[slot][0:1, :] - mean
        values = jnp.where(real, seen - mean, jnp.where(row_id == m, innov, 0.0))
        return values.astype(BF16)

    def term(values, weights, slot):
        strip_rows = [weights[pl.ds(slot * strips + i, 1), :] for i in range(strips)]
        scale = jnp.concatenate(strip_rows, axis=1)
        return dot_t((values.astype(F32) * scale).astype(BF16), values)

    tables = (wbuf.at[0], wbuf.at[1], wd.at[pl.ds(block, block)])
    for k in range(2):
        slot = take(k)
        if k == 0:
            for copy in (y_up, y_down, w_left, w_right):
                copy.wait_recv()
        values = perturbed(slot)
        for i, table in enumerate(tables):
            if k == 0:
                gacc[i] = term(values, table, slot)
            else:
                gacc[i] += term(values, table, slot)
        if k == 0:
            for dest in state_later:
                state_copies.append(state_send(dest, len(state_copies)))
    slot = take(2)

    values = perturbed(slot)
    gsend[0] = (gacc[0] + term(values, tables[0], slot)).astype(BF16)
    g_right = send(gsend.at[0], grecv.at[0], g_ss.at[0], g_rs.at[0], (me, right))
    gsend[1] = (gacc[1] + term(values, tables[1], slot)).astype(BF16)
    g_left = send(gsend.at[1], grecv.at[1], g_ss.at[1], g_rs.at[1], (me, left))
    own = gacc[2] + term(values, tables[2], slot)
    g_right.wait_recv()
    g_left.wait_recv()
    full = own + (grecv[0].astype(F32) + grecv[1].astype(F32))

    col_id = lax.broadcasted_iota(jnp.int32, (1, total), 1)
    real_col = lax.rem(col_id, pad) < m
    same = row_id == col_id
    eye = jnp.where(same, 1.0, 0.0)
    drive = jnp.where(real_col, full[m:m + 1, :], 0.0)
    gram = jnp.where(real & real_col, full, 0.0)
    gram = gram + jnp.where(same & real, (members - 1) / INFLATION, 0.0)
    norm = jnp.sqrt(jnp.sum(jnp.sum(gram * gram, axis=0, keepdims=True), axis=1, keepdims=True))
    root = newton(gram, norm, eye, NS_STEPS)
    product = jnp.sum(root * drive, axis=1, keepdims=True)
    shift = jnp.sum(root * product, axis=0, keepdims=True)
    wt[...] = (math.sqrt(members - 1) / jnp.sqrt(norm) * root + shift / norm).astype(BF16)

    for d in range(1, n):
        pltpu.make_async_remote_copy(
            src_ref=bgp.at[0], dst_ref=sbuf.at[peer(d)], send_sem=st_ss.at[0], recv_sem=st_rs.at[peer(d)],
            device_id=(peer(d), col), device_id_type=MESH,
        ).wait_recv()
    states = sbuf[...].reshape(total, cells).astype(F32)
    state_mean = jnp.sum(states, axis=0, keepdims=True) / members
    state_pert = jnp.where(real, states - state_mean, 0.0).astype(BF16)

    out_copies = []
    if n == 4:
        dests = [turn(3, 3), turn(2, 3), turn(other, 3)]
    else:
        dests = [peer(d) for d in range(n - 1, 0, -1)]
    for d, dest in enumerate(dests + [me]):
        rows = wt[pl.ds(pl.multiple_of(dest * pad, 16), pad), :]
        result = (state_mean + jnp.dot(rows, state_pert, preferred_element_type=F32)).astype(BF16)
        if d == n - 1:
            oland[me] = result
        else:
            oloc[d] = result
            out_copies.append(
                send(oloc.at[d], oland.at[me], o_ss.at[d], o_rs.at[me], (dest, col))
            )

    def finish(source):
        out_ref[:, pl.ds(pl.multiple_of(source * cells, 128), cells)] = oland[source, 0:m, :]

    finish(me)
    for source in reversed(dests):
        pltpu.make_async_remote_copy(
            src_ref=oloc.at[0], dst_ref=oland.at[source], send_sem=o_ss.at[0], recv_sem=o_rs.at[source],
            device_id=(source, col), device_id_type=MESH,
        ).wait_recv()
        finish(source)
    for copy in obs_copies + state_copies + out_copies:
        copy.wait_send()
    for copy in (w_left, w_right, y_up, y_down, g_right, g_left):
        copy.wait_send()
    if n == 4:
        @pl.when(inner)
        def _():
            for i, (source, slot) in enumerate(handed):
                hand_on(i, source, slot).wait_send()


def local(background, obs_index, yobs, loc_list, loc_count, loc_weight):
    n, regs = lax.axis_size("mem"), lax.axis_size("reg")
    m = background.shape[0]
    rows, width = obs_index.shape[1], obs_index.shape[2]
    cells = background.shape[2] // rows
    length = loc_list.shape[2]
    pad = (m // 16 + 1) * 16
    total = n * pad
    block = -(-3 * (width // 128) // 8) * 8
    vmem = pl.BlockSpec(memory_space=pltpu.VMEM)
    dma = pltpu.SemaphoreType.DMA
    result = pl.pallas_call(
        functools.partial(kernel, n, regs, m, pad, width, cells),
        out_shape=jax.ShapeDtypeStruct((m, rows * cells), BF16),
        in_specs=[pl.BlockSpec(memory_space=pltpu.HBM)] * 5 + [pl.BlockSpec(memory_space=pltpu.SMEM)],
        out_specs=vmem,
        scratch_shapes=[
            pltpu.VMEM((m, rows * cells), BF16),
            pltpu.VMEM((rows, width), jnp.int32),
            pltpu.VMEM((1, width), BF16),
            pltpu.VMEM((1, length), jnp.int32),
            pltpu.VMEM((1, length), F32),
            pltpu.VMEM((n, pad, cells), BF16),
            pltpu.VMEM((n, pad, width), BF16),
            pltpu.VMEM((n, 3, pad, width), BF16),
            pltpu.VMEM((n, pad, cells), BF16),
            pltpu.VMEM((3 * block, 128), F32),
            pltpu.VMEM((2, block, 128), F32),
            pltpu.VMEM((8, width), F32),
            pltpu.VMEM((3, 8, width), F32),
            pltpu.VMEM((3, total, total), F32),
            pltpu.VMEM((2, total, total), BF16),
            pltpu.VMEM((2, total, total), BF16),
            pltpu.VMEM((total, total), BF16),
            pltpu.VMEM((n, pad, cells), BF16),
            pltpu.VMEM((n, pad, cells), BF16),
            dma((3 * n,)), dma((n, 3)),
            dma((n,)), dma((n,)),
            dma((2,)), dma((2,)),
            dma((2,)), dma((2,)),
            dma((2,)), dma((2,)),
            dma((n,)), dma((n,)), dma((5,)),
        ],
        compiler_params=pltpu.CompilerParams(
            collective_id=0, has_side_effects=True, vmem_limit_bytes=40 * 1024 * 1024
        ),
    )(
        *(
            pltpu.with_memory_space_constraint(x, pltpu.HBM)
            for x in (
                background.reshape(m, rows * cells),
                obs_index.reshape(rows, width),
                yobs.reshape(1, width),
                loc_list.reshape(1, length),
                loc_weight.reshape(1, length),
            )
        ),
        loc_count.reshape(1, 1),
    )
    return result.reshape(m, 1, rows * cells)


def solution(mesh):
    return jax.shard_map(
        local,
        mesh=mesh,
        in_specs=(
            P("mem", "reg", None),
            P("reg", None, None),
            P("reg", "mem", None),
            P("reg", "mem", None),
            P("reg", "mem"),
            P("reg", "mem", None),
        ),
        out_specs=P("mem", "reg", None),
        check_vma=False,
    )
```

```python
import functools
import math

import jax
import jax.numpy as jnp
from jax import lax
from jax.experimental import pallas as pl
from jax.experimental.pallas import tpu as pltpu
from jax.sharding import PartitionSpec as P

NS_STEPS = 5
INFLATION = 1.1
MESH = pl.DeviceIdType.MESH
F32 = jnp.float32
BF16 = jnp.bfloat16


def split(x):
    high = x.astype(BF16)
    return high, (x - high.astype(F32)).astype(BF16)


def mm(a, b, passes):
    top = jnp.dot(a[0], b[0], preferred_element_type=F32)
    if passes == 1:
        return top
    return (
        jnp.dot(a[0], b[1], preferred_element_type=F32)
        + jnp.dot(a[1], b[0], preferred_element_type=F32)
        + top
    )


def dot_t(a, b):
    return lax.dot_general(a, b, (((1,), (1,)), ((), ())), preferred_element_type=F32)


def newton(gram, norm, eye, steps):
    t = gram * (1.0 / norm)
    root = None
    for step in range(steps):
        passes = 1 if step < steps - 2 else 3
        t_s = split(t)
        if root is None:
            root = 1.5 * eye - 0.5 * t
        else:
            root = 1.5 * root - 0.5 * mm(t_s, split(root), passes)
        if step < steps - 1:
            square = mm(t_s, t_s, passes)
            t = 2.25 * t - 1.5 * square + 0.25 * mm(t_s, split(square), passes)
    return root


def packed_shape(m, pad, width):
    rest = m % 16
    base = m - rest
    if rest and base and base % rest == 0 and (width * rest // base) % 128 == 0 and width * rest % base == 0:
        return base, width + width * rest // base
    return pad, width


def pack(x, m, shape):
    base, lanes = shape
    width = x.shape[1]
    if lanes == width:
        return x.astype(BF16)
    extra = lanes - width
    rest = jnp.concatenate([x[base:m, i:i + extra] for i in range(0, width, extra)], axis=0)
    return jnp.concatenate([x[:base], rest], axis=1).astype(BF16)


def unpack(y, m, pad, width):
    y = y.astype(F32)
    if y.shape[1] == width:
        return y
    rest = m - y.shape[0]
    tail = jnp.concatenate([y[i:i + rest, width:] for i in range(0, y.shape[0], rest)], axis=1)
    return jnp.concatenate([y[:, :width], tail, jnp.zeros((pad - m, width), F32)], axis=0)


def kernel(
    n, regs, m, pad, width, cells,
    bg_hbm, idx_hbm, yobs_hbm, list_hbm, weight_hbm, count_ref,
    out_ref,
    bg_ref, idx_ref, yobs_ref, list_ref, weight_ref,
    bgp, spack, obs_loc, obuf, sbuf, wd, wbuf, yloc, ybuf, gacc, gsend, grecv, wt, oloc, oland,
    obs_ss, obs_rs, st_ss, st_rs, w_ss, w_rs, y_ss, y_rs, g_ss, g_rs, o_ss, o_rs, in_sem,
):
    me, col = lax.axis_index("mem"), lax.axis_index("reg")
    left, right = lax.rem(col + regs - 1, regs), lax.rem(col + 1, regs)
    members, total = n * m, n * pad
    lanes = 128
    strips = width // lanes
    block = wd.shape[0] // 3

    def peer(d):
        return lax.rem(me + d, n)

    barrier = pltpu.get_barrier_semaphore()
    for d in range(1, n):
        pl.semaphore_signal(barrier, inc=1, device_id=(peer(d), col), device_id_type=MESH)
    for c in (left, right):
        pl.semaphore_signal(barrier, inc=1, device_id=(me, c), device_id_type=MESH)

    def send(src, dst, ss, rs, device):
        copy = pltpu.make_async_remote_copy(
            src_ref=src, dst_ref=dst, send_sem=ss, recv_sem=rs,
            device_id=device, device_id_type=MESH,
        )
        copy.start()
        return copy

    loads = [
        pltpu.make_async_copy(src, dst, in_sem.at[i])
        for i, (src, dst) in enumerate((
            (bg_hbm, bg_ref), (idx_hbm, idx_ref), (yobs_hbm, yobs_ref),
            (list_hbm, list_ref), (weight_hbm, weight_ref),
        ))
    ]
    for load in loads:
        load.start()

    for load in loads[:3]:
        load.wait()
    tail = (m // 16) * 16
    for q in range(n):
        bgp[q, tail:pad, :] = jnp.zeros((pad - tail, cells), BF16)
        bgp[q, 0:m, :] = bg_ref[:, q * cells:(q + 1) * cells]

    yloc[...] = jnp.broadcast_to(yobs_ref[...].astype(F32), yloc.shape)
    ybuf[1] = yloc[...]

    pl.semaphore_wait(barrier, n + 1)

    y_up = send(yloc, ybuf.at[0], y_ss.at[0], y_rs.at[0], (peer(1), col))
    y_down = send(yloc, ybuf.at[2], y_ss.at[1], y_rs.at[1], (peer(n - 1), col))

    def observe(row):
        hot = lax.broadcasted_iota(jnp.int32, (cells, width), 0) == idx_ref[pl.ds(row, 1), :]
        hot = jnp.where(hot, 1.0, 0.0).astype(BF16)
        seen = jnp.dot(bgp[row], hot, preferred_element_type=F32)
        return pack(seen, m, obs_loc.shape[1:])

    obs_copies = []
    if n == 4:
        side = me // 2

        def turn(x, last):
            return x + side * (last - 2 * x)

        here = turn(me, 3)
        inner = here == 1
        other = 1 - here

        def obs_send(row, dest, slot, i):
            return send(
                obs_loc.at[row], obuf.at[me, turn(slot, 2)], obs_ss.at[i],
                obs_rs.at[me, turn(slot, 2)], (turn(dest, 3), col),
            )

        def landed(source, slot):
            return pltpu.make_async_remote_copy(
                src_ref=obs_loc.at[0], dst_ref=obuf.at[turn(source, 3), turn(slot, 2)],
                send_sem=obs_ss.at[0], recv_sem=obs_rs.at[turn(source, 3), turn(slot, 2)],
                device_id=(turn(other, 3), col), device_id_type=MESH,
            )

        for i, (row, dest, slot) in enumerate(((2, 2, 1), (3, 2, 2), (1, 2, 0), (0, 3, 2))):
            obs_loc[row] = observe(turn(row, 3))
            obs_copies.append(obs_send(row, dest, slot, i))
        def kth(place, k):
            return (2 - place, 1 - place, 2 * place)[k]

        for k in range(3):
            slot = kth(other, k)
            obs_copies.append(obs_send(lax.rem(other + slot + 3, 4), other, slot, 4 + k))
        for slot in range(3):
            obuf[me, turn(slot, 2)] = obs_loc[lax.rem(here + slot + 3, 4)]

        handed = ((2, 1), (2, 0), (3, 1), (3, 0))

        def hand_on(i, source, slot):
            return pltpu.make_async_remote_copy(
                src_ref=obuf.at[turn(source, 3), turn(slot, 2)],
                dst_ref=obuf.at[turn(source, 3), turn(slot + 1, 2)],
                send_sem=obs_ss.at[7 + i], recv_sem=obs_rs.at[turn(source, 3), turn(slot + 1, 2)],
                device_id=(turn(0, 3), col), device_id_type=MESH,
            )
    else:
        for t in sorted(range(n), key=lambda t: -min(t, n - t)):
            obs_loc[t] = observe(peer(t))
            for slot in (0, 1, 2):
                d = (t + 1 - slot) % n
                if d == 0:
                    obuf[me, slot] = obs_loc[t]
                else:
                    obs_copies.append(
                        send(
                            obs_loc.at[t], obuf.at[me, slot], obs_ss.at[3 * d + slot],
                            obs_rs.at[d, slot], (peer(d), col),
                        )
                    )

    for load in loads[3:]:
        load.wait()
    length = list_ref.shape[1]
    place = lax.broadcasted_iota(jnp.int32, (1, length), 1)
    live = jnp.where(place < count_ref[0, 0], weight_ref[...], 0.0)
    part0 = live.astype(BF16)
    rest = live - part0.astype(F32)
    part1 = rest.astype(BF16)
    part2 = (rest - part1.astype(F32)).astype(BF16)
    cand = list_ref[...]
    strip = cand // lanes
    lane = cand - strip * lanes
    group = strip // (3 * strips)
    strip = strip + group * (block - 3 * strips)
    rows_at = lax.broadcasted_iota(jnp.int32, (3 * block, length), 0) == strip
    lanes_at = lax.broadcasted_iota(jnp.int32, (lanes, length), 0) == lane
    lane_hot = jnp.where(lanes_at, 1.0, 0.0).astype(BF16)
    spread = [
        dot_t(jnp.where(rows_at, part.astype(F32), 0.0).astype(BF16), lane_hot)
        for part in (part0, part1, part2)
    ]
    wd[...] = spread[0] + (spread[1] + spread[2])
    w_left = send(wd.at[pl.ds(0, block)], wbuf.at[0], w_ss.at[0], w_rs.at[0], (me, left))
    w_right = send(wd.at[pl.ds(2 * block, block)], wbuf.at[1], w_ss.at[1], w_rs.at[1], (me, right))

    def state_send(dest, i):
        return send(spack.at[dest], sbuf.at[me], st_ss.at[i], st_rs.at[me], (dest, col))

    for q in range(n):
        spack[q] = pack(bgp[q].astype(F32), m, spack.shape[1:])
    sbuf[me] = spack[me]
    if n == 4:
        state_copies = [state_send(turn(2, 3), 0)]
        state_later = [turn(3, 3), turn(other, 3)]
    else:
        state_copies = []
        state_later = [peer(d) for d in range(n - 1, 0, -1)]

    if n == 4:
        @pl.when(inner)
        def _():
            for i, (source, slot) in enumerate(handed):
                landed(source, slot).wait_recv()
                hand_on(i, source, slot).start()

    def take(k):
        if n != 4:
            if k == 0:
                for copy in obs_copies:
                    copy.wait_recv()
            return k
        slot = kth(here, k)
        if k == 2:
            for source in (2, 3):
                landed(source, slot).wait_recv()
        else:
            @pl.when(jnp.logical_not(inner))
            def _():
                for source in (2, 3):
                    landed(source, slot).wait_recv()
        landed(other, slot).wait_recv()
        return turn(slot, 2)

    row_id = lax.broadcasted_iota(jnp.int32, (total, 1), 0)
    real = lax.rem(row_id, pad) < m

    def perturbed(slot):
        seen = jnp.concatenate([unpack(obuf[z, slot], m, pad, width) for z in range(n)], axis=0)
        mean = jnp.sum(seen, axis=0, keepdims=True) / members
        innov = ybuf[slot][0:1, :] - mean
        values = jnp.where(real, seen - mean, jnp.where(row_id == m, innov, 0.0))
        return values.astype(BF16)

    def term(values, weights, slot):
        strip_rows = [weights[pl.ds(slot * strips + i, 1), :] for i in range(strips)]
        scale = jnp.concatenate(strip_rows, axis=1)
        return dot_t((values.astype(F32) * scale).astype(BF16), values)

    tables = (wbuf.at[0], wbuf.at[1], wd.at[pl.ds(block, block)])
    for k in range(2):
        slot = take(k)
        if k == 0:
            for copy in (y_up, y_down, w_left, w_right):
                copy.wait_recv()
        values = perturbed(slot)
        for i, table in enumerate(tables):
            if k == 0:
                gacc[i] = term(values, table, slot)
            else:
                gacc[i] += term(values, table, slot)
        if k == 0:
            for dest in state_later:
                state_copies.append(state_send(dest, len(state_copies)))
    slot = take(2)

    values = perturbed(slot)
    gsend[0] = (gacc[0] + term(values, tables[0], slot)).astype(BF16)
    g_right = send(gsend.at[0], grecv.at[0], g_ss.at[0], g_rs.at[0], (me, right))
    gsend[1] = (gacc[1] + term(values, tables[1], slot)).astype(BF16)
    g_left = send(gsend.at[1], grecv.at[1], g_ss.at[1], g_rs.at[1], (me, left))
    own = gacc[2] + term(values, tables[2], slot)
    g_right.wait_recv()
    g_left.wait_recv()
    full = own + (grecv[0].astype(F32) + grecv[1].astype(F32))

    col_id = lax.broadcasted_iota(jnp.int32, (1, total), 1)
    real_col = lax.rem(col_id, pad) < m
    same = row_id == col_id
    eye = jnp.where(same, 1.0, 0.0)
    drive = jnp.where(real_col, full[m:m + 1, :], 0.0)
    gram = jnp.where(real & real_col, full, 0.0)
    gram = gram + jnp.where(same & real, (members - 1) / INFLATION, 0.0)
    norm = jnp.sqrt(jnp.sum(jnp.sum(gram * gram, axis=0, keepdims=True), axis=1, keepdims=True))
    root = newton(gram, norm, eye, NS_STEPS)
    product = jnp.sum(root * drive, axis=1, keepdims=True)
    shift = jnp.sum(root * product, axis=0, keepdims=True)
    wt[...] = (math.sqrt(members - 1) / jnp.sqrt(norm) * root + shift / norm).astype(BF16)

    for d in range(1, n):
        pltpu.make_async_remote_copy(
            src_ref=spack.at[0], dst_ref=sbuf.at[peer(d)], send_sem=st_ss.at[0], recv_sem=st_rs.at[peer(d)],
            device_id=(peer(d), col), device_id_type=MESH,
        ).wait_recv()
    states = jnp.concatenate([unpack(sbuf[z], m, pad, cells) for z in range(n)], axis=0)
    state_mean = jnp.sum(states, axis=0, keepdims=True) / members
    state_pert = jnp.where(real, states - state_mean, 0.0).astype(BF16)

    out_copies = []
    if n == 4:
        dests = [turn(3, 3), turn(2, 3), turn(other, 3)]
    else:
        dests = [peer(d) for d in range(n - 1, 0, -1)]
    for d, dest in enumerate(dests + [me]):
        rows = wt[pl.ds(pl.multiple_of(dest * pad, 16), pad), :]
        result = (state_mean + jnp.dot(rows, state_pert, preferred_element_type=F32))
        result = pack(result, m, oloc.shape[1:])
        if d == n - 1:
            oland[me] = result
        else:
            oloc[d] = result
            out_copies.append(
                send(oloc.at[d], oland.at[me], o_ss.at[d], o_rs.at[me], (dest, col))
            )

    def finish(source):
        out_ref[:, pl.ds(pl.multiple_of(source * cells, 128), cells)] = unpack(oland[source], m, pad, cells)[0:m].astype(BF16)

    finish(me)
    for source in reversed(dests):
        pltpu.make_async_remote_copy(
            src_ref=oloc.at[0], dst_ref=oland.at[source], send_sem=o_ss.at[0], recv_sem=o_rs.at[source],
            device_id=(source, col), device_id_type=MESH,
        ).wait_recv()
        finish(source)
    for copy in obs_copies + state_copies + out_copies:
        copy.wait_send()
    for copy in (w_left, w_right, y_up, y_down, g_right, g_left):
        copy.wait_send()
    if n == 4:
        @pl.when(inner)
        def _():
            for i, (source, slot) in enumerate(handed):
                hand_on(i, source, slot).wait_send()


def local(background, obs_index, yobs, loc_list, loc_count, loc_weight):
    n, regs = lax.axis_size("mem"), lax.axis_size("reg")
    m = background.shape[0]
    rows, width = obs_index.shape[1], obs_index.shape[2]
    cells = background.shape[2] // rows
    length = loc_list.shape[2]
    pad = (m // 16 + 1) * 16
    total = n * pad
    block = -(-3 * (width // 128) // 8) * 8
    obs_block, state_block = packed_shape(m, pad, width), packed_shape(m, pad, cells)
    vmem = pl.BlockSpec(memory_space=pltpu.VMEM)
    dma = pltpu.SemaphoreType.DMA
    result = pl.pallas_call(
        functools.partial(kernel, n, regs, m, pad, width, cells),
        out_shape=jax.ShapeDtypeStruct((m, rows * cells), BF16),
        in_specs=[pl.BlockSpec(memory_space=pltpu.HBM)] * 5 + [pl.BlockSpec(memory_space=pltpu.SMEM)],
        out_specs=vmem,
        scratch_shapes=[
            pltpu.VMEM((m, rows * cells), BF16),
            pltpu.VMEM((rows, width), jnp.int32),
            pltpu.VMEM((1, width), BF16),
            pltpu.VMEM((1, length), jnp.int32),
            pltpu.VMEM((1, length), F32),
            pltpu.VMEM((n, pad, cells), BF16),
            pltpu.VMEM((n, *state_block), BF16),
            pltpu.VMEM((n, *obs_block), BF16),
            pltpu.VMEM((n, 3, *obs_block), BF16),
            pltpu.VMEM((n, *state_block), BF16),
            pltpu.VMEM((3 * block, 128), F32),
            pltpu.VMEM((2, block, 128), F32),
            pltpu.VMEM((8, width), F32),
            pltpu.VMEM((3, 8, width), F32),
            pltpu.VMEM((3, total, total), F32),
            pltpu.VMEM((2, total, total), BF16),
            pltpu.VMEM((2, total, total), BF16),
            pltpu.VMEM((total, total), BF16),
            pltpu.VMEM((n, *state_block), BF16),
            pltpu.VMEM((n, *state_block), BF16),
            dma((3 * n,)), dma((n, 3)),
            dma((n,)), dma((n,)),
            dma((2,)), dma((2,)),
            dma((2,)), dma((2,)),
            dma((2,)), dma((2,)),
            dma((n,)), dma((n,)), dma((5,)),
        ],
        compiler_params=pltpu.CompilerParams(
            collective_id=0, has_side_effects=True, vmem_limit_bytes=40 * 1024 * 1024
        ),
    )(
        *(
            pltpu.with_memory_space_constraint(x, pltpu.HBM)
            for x in (
                background.reshape(m, rows * cells),
                obs_index.reshape(rows, width),
                yobs.reshape(1, width),
                loc_list.reshape(1, length),
                loc_weight.reshape(1, length),
            )
        ),
        loc_count.reshape(1, 1),
    )
    return result.reshape(m, 1, rows * cells)


def solution(mesh):
    return jax.shard_map(
        local,
        mesh=mesh,
        in_specs=(
            P("mem", "reg", None),
            P("reg", None, None),
            P("reg", "mem", None),
            P("reg", "mem", None),
            P("reg", "mem"),
            P("reg", "mem", None),
        ),
        out_specs=P("mem", "reg", None),
        check_vma=False,
    )
```

```python
import functools
import math

import jax
import jax.numpy as jnp
from jax import lax
from jax.experimental import pallas as pl
from jax.experimental.pallas import tpu as pltpu
from jax.sharding import PartitionSpec as P

NS_STEPS = 5
INFLATION = 1.1
MESH = pl.DeviceIdType.MESH
F32 = jnp.float32
BF16 = jnp.bfloat16


def split(x):
    high = x.astype(BF16)
    return high, (x - high.astype(F32)).astype(BF16)


def mm(a, b, passes):
    top = jnp.dot(a[0], b[0], preferred_element_type=F32)
    if passes == 1:
        return top
    return (
        jnp.dot(a[0], b[1], preferred_element_type=F32)
        + jnp.dot(a[1], b[0], preferred_element_type=F32)
        + top
    )


def dot_t(a, b):
    return lax.dot_general(a, b, (((1,), (1,)), ((), ())), preferred_element_type=F32)


def newton(gram, norm, eye, steps):
    t = gram * (1.0 / norm)
    root = None
    for step in range(steps):
        passes = 1 if step < steps - 2 else 3
        t_s = split(t)
        if root is None:
            root = 1.5 * eye - 0.5 * t
        else:
            root = 1.5 * root - 0.5 * mm(t_s, split(root), passes)
        if step < steps - 1:
            square = mm(t_s, t_s, passes)
            t = 2.25 * t - 1.5 * square + 0.25 * mm(t_s, split(square), passes)
    return root


def packed_shape(m, pad, width):
    rest = m % 16
    base = m - rest
    if rest and base and base % rest == 0 and (width * rest // base) % 128 == 0 and width * rest % base == 0:
        return base, width + width * rest // base
    return pad, width


def pack(x, m, shape):
    base, lanes = shape
    width = x.shape[1]
    if lanes == width:
        return x.astype(BF16)
    extra = lanes - width
    rest = jnp.concatenate([x[base:m, i:i + extra] for i in range(0, width, extra)], axis=0)
    return jnp.concatenate([x[:base], rest], axis=1).astype(BF16)


def unpack(y, m, pad, width):
    y = y.astype(F32)
    if y.shape[1] == width:
        return y
    rest = m - y.shape[0]
    tail = jnp.concatenate([y[i:i + rest, width:] for i in range(0, y.shape[0], rest)], axis=1)
    return jnp.concatenate([y[:, :width], tail, jnp.zeros((pad - m, width), F32)], axis=0)


def kernel(
    n, regs, m, pad, width, cells,
    bg_hbm, idx_hbm, yobs_hbm, list_hbm, weight_hbm, count_ref,
    out_ref,
    bg_ref, idx_ref, yobs_ref, list_ref, weight_ref,
    bgp, spack, obs_loc, obuf, sbuf, wd, wbuf, yloc, ybuf, gacc, gsend, grecv, wt, oloc, oland,
    obs_ss, obs_rs, st_ss, st_rs, w_ss, w_rs, y_ss, y_rs, g_ss, g_rs, o_ss, o_rs, in_sem,
):
    me, col = lax.axis_index("mem"), lax.axis_index("reg")
    left, right = lax.rem(col + regs - 1, regs), lax.rem(col + 1, regs)
    members, total = n * m, n * pad
    lanes = 128
    strips = width // lanes
    block = wd.shape[0] // 3

    def peer(d):
        return lax.rem(me + d, n)

    barrier = pltpu.get_barrier_semaphore()
    for d in range(1, n):
        pl.semaphore_signal(barrier, inc=1, device_id=(peer(d), col), device_id_type=MESH)
    for c in (left, right):
        pl.semaphore_signal(barrier, inc=1, device_id=(me, c), device_id_type=MESH)

    def send(src, dst, ss, rs, device):
        copy = pltpu.make_async_remote_copy(
            src_ref=src, dst_ref=dst, send_sem=ss, recv_sem=rs,
            device_id=device, device_id_type=MESH,
        )
        copy.start()
        return copy

    loads = [
        pltpu.make_async_copy(src, dst, in_sem.at[i])
        for i, (src, dst) in enumerate((
            (bg_hbm, bg_ref), (idx_hbm, idx_ref), (yobs_hbm, yobs_ref),
            (list_hbm, list_ref), (weight_hbm, weight_ref),
        ))
    ]
    for load in loads:
        load.start()

    for load in loads[:3]:
        load.wait()
    tail = (m // 16) * 16

    def fill(q):
        bgp[q, tail:pad, :] = jnp.zeros((pad - tail, cells), BF16)
        bgp[q, 0:m, :] = bg_ref[:, pl.ds(pl.multiple_of(q * cells, 128), cells)]

    yloc[...] = jnp.broadcast_to(yobs_ref[...].astype(F32), yloc.shape)
    ybuf[1] = yloc[...]

    pl.semaphore_wait(barrier, n + 1)

    y_up = send(yloc, ybuf.at[0], y_ss.at[0], y_rs.at[0], (peer(1), col))
    y_down = send(yloc, ybuf.at[2], y_ss.at[1], y_rs.at[1], (peer(n - 1), col))

    def observe(row):
        hot = lax.broadcasted_iota(jnp.int32, (cells, width), 0) == idx_ref[pl.ds(row, 1), :]
        hot = jnp.where(hot, 1.0, 0.0).astype(BF16)
        fill(row)
        seen = jnp.dot(bgp[row], hot, preferred_element_type=F32)
        return pack(seen, m, obs_loc.shape[1:])

    obs_copies = []
    if n == 4:
        side = me // 2

        def turn(x, last):
            return x + side * (last - 2 * x)

        here = turn(me, 3)
        inner = here == 1
        other = 1 - here

        def obs_send(row, dest, slot, i):
            return send(
                obs_loc.at[row], obuf.at[me, turn(slot, 2)], obs_ss.at[i],
                obs_rs.at[me, turn(slot, 2)], (turn(dest, 3), col),
            )

        def landed(source, slot):
            return pltpu.make_async_remote_copy(
                src_ref=obs_loc.at[0], dst_ref=obuf.at[turn(source, 3), turn(slot, 2)],
                send_sem=obs_ss.at[0], recv_sem=obs_rs.at[turn(source, 3), turn(slot, 2)],
                device_id=(turn(other, 3), col), device_id_type=MESH,
            )

        for i, (row, dest, slot) in enumerate(((2, 2, 1), (3, 2, 2), (1, 2, 0), (0, 3, 2))):
            obs_loc[row] = observe(turn(row, 3))
            obs_copies.append(obs_send(row, dest, slot, i))
        def kth(place, k):
            return (2 - place, 1 - place, 2 * place)[k]

        for k in range(3):
            slot = kth(other, k)
            obs_copies.append(obs_send(lax.rem(other + slot + 3, 4), other, slot, 4 + k))
        for slot in range(3):
            obuf[me, turn(slot, 2)] = obs_loc[lax.rem(here + slot + 3, 4)]

        handed = ((2, 1), (2, 0), (3, 1), (3, 0))

        def hand_on(i, source, slot):
            return pltpu.make_async_remote_copy(
                src_ref=obuf.at[turn(source, 3), turn(slot, 2)],
                dst_ref=obuf.at[turn(source, 3), turn(slot + 1, 2)],
                send_sem=obs_ss.at[7 + i], recv_sem=obs_rs.at[turn(source, 3), turn(slot + 1, 2)],
                device_id=(turn(0, 3), col), device_id_type=MESH,
            )
    else:
        for t in sorted(range(n), key=lambda t: -min(t, n - t)):
            obs_loc[t] = observe(peer(t))
            for slot in (0, 1, 2):
                d = (t + 1 - slot) % n
                if d == 0:
                    obuf[me, slot] = obs_loc[t]
                else:
                    obs_copies.append(
                        send(
                            obs_loc.at[t], obuf.at[me, slot], obs_ss.at[3 * d + slot],
                            obs_rs.at[d, slot], (peer(d), col),
                        )
                    )

    for load in loads[3:]:
        load.wait()
    length = list_ref.shape[1]
    place = lax.broadcasted_iota(jnp.int32, (1, length), 1)
    live = jnp.where(place < count_ref[0, 0], weight_ref[...], 0.0)
    part0 = live.astype(BF16)
    rest = live - part0.astype(F32)
    part1 = rest.astype(BF16)
    part2 = (rest - part1.astype(F32)).astype(BF16)
    cand = list_ref[...]
    strip = cand // lanes
    lane = cand - strip * lanes
    group = strip // (3 * strips)
    strip = strip + group * (block - 3 * strips)
    rows_at = lax.broadcasted_iota(jnp.int32, (3 * block, length), 0) == strip
    lanes_at = lax.broadcasted_iota(jnp.int32, (lanes, length), 0) == lane
    lane_hot = jnp.where(lanes_at, 1.0, 0.0).astype(BF16)
    spread = [
        dot_t(jnp.where(rows_at, part.astype(F32), 0.0).astype(BF16), lane_hot)
        for part in (part0, part1, part2)
    ]
    wd[...] = spread[0] + (spread[1] + spread[2])
    w_left = send(wd.at[pl.ds(0, block)], wbuf.at[0], w_ss.at[0], w_rs.at[0], (me, left))
    w_right = send(wd.at[pl.ds(2 * block, block)], wbuf.at[1], w_ss.at[1], w_rs.at[1], (me, right))

    def state_send(dest, i):
        return send(spack.at[dest], sbuf.at[me], st_ss.at[i], st_rs.at[me], (dest, col))

    for q in range(n):
        spack[q] = pack(bgp[q].astype(F32), m, spack.shape[1:])
    sbuf[me] = spack[me]
    if n == 4:
        state_copies = [state_send(turn(2, 3), 0)]
        state_later = [turn(3, 3), turn(other, 3)]
    else:
        state_copies = []
        state_later = [peer(d) for d in range(n - 1, 0, -1)]

    if n == 4:
        @pl.when(inner)
        def _():
            for i, (source, slot) in enumerate(handed):
                landed(source, slot).wait_recv()
                hand_on(i, source, slot).start()

    def take(k):
        if n != 4:
            if k == 0:
                for copy in obs_copies:
                    copy.wait_recv()
            return k
        slot = kth(here, k)
        if k == 2:
            for source in (2, 3):
                landed(source, slot).wait_recv()
        else:
            @pl.when(jnp.logical_not(inner))
            def _():
                for source in (2, 3):
                    landed(source, slot).wait_recv()
        landed(other, slot).wait_recv()
        return turn(slot, 2)

    row_id = lax.broadcasted_iota(jnp.int32, (total, 1), 0)
    real = lax.rem(row_id, pad) < m

    def perturbed(slot):
        seen = jnp.concatenate([unpack(obuf[z, slot], m, pad, width) for z in range(n)], axis=0)
        mean = jnp.sum(seen, axis=0, keepdims=True) / members
        innov = ybuf[slot][0:1, :] - mean
        values = jnp.where(real, seen - mean, jnp.where(row_id == m, innov, 0.0))
        return values.astype(BF16)

    def term(values, weights, slot):
        strip_rows = [weights[pl.ds(slot * strips + i, 1), :] for i in range(strips)]
        scale = jnp.concatenate(strip_rows, axis=1)
        return dot_t((values.astype(F32) * scale).astype(BF16), values)

    tables = (wbuf.at[0], wbuf.at[1], wd.at[pl.ds(block, block)])
    for k in range(2):
        slot = take(k)
        if k == 0:
            for copy in (y_up, y_down, w_left, w_right):
                copy.wait_recv()
        values = perturbed(slot)
        for i, table in enumerate(tables):
            if k == 0:
                gacc[i] = term(values, table, slot)
            else:
                gacc[i] += term(values, table, slot)
        if k == 0:
            for dest in state_later:
                state_copies.append(state_send(dest, len(state_copies)))
    slot = take(2)

    values = perturbed(slot)
    gsend[0] = (gacc[0] + term(values, tables[0], slot)).astype(BF16)
    g_right = send(gsend.at[0], grecv.at[0], g_ss.at[0], g_rs.at[0], (me, right))
    gsend[1] = (gacc[1] + term(values, tables[1], slot)).astype(BF16)
    g_left = send(gsend.at[1], grecv.at[1], g_ss.at[1], g_rs.at[1], (me, left))
    own = gacc[2] + term(values, tables[2], slot)
    g_right.wait_recv()
    g_left.wait_recv()
    full = own + (grecv[0].astype(F32) + grecv[1].astype(F32))

    col_id = lax.broadcasted_iota(jnp.int32, (1, total), 1)
    real_col = lax.rem(col_id, pad) < m
    same = row_id == col_id
    eye = jnp.where(same, 1.0, 0.0)
    drive = jnp.where(real_col, full[m:m + 1, :], 0.0)
    gram = jnp.where(real & real_col, full, 0.0)
    gram = gram + jnp.where(same & real, (members - 1) / INFLATION, 0.0)
    norm = jnp.sqrt(jnp.sum(jnp.sum(gram * gram, axis=0, keepdims=True), axis=1, keepdims=True))
    root = newton(gram, norm, eye, NS_STEPS)
    product = jnp.sum(root * drive, axis=1, keepdims=True)
    shift = jnp.sum(root * product, axis=0, keepdims=True)
    wt[...] = (math.sqrt(members - 1) / jnp.sqrt(norm) * root + shift / norm).astype(BF16)

    for d in range(1, n):
        pltpu.make_async_remote_copy(
            src_ref=spack.at[0], dst_ref=sbuf.at[peer(d)], send_sem=st_ss.at[0], recv_sem=st_rs.at[peer(d)],
            device_id=(peer(d), col), device_id_type=MESH,
        ).wait_recv()
    states = jnp.concatenate([unpack(sbuf[z], m, pad, cells) for z in range(n)], axis=0)
    state_mean = jnp.sum(states, axis=0, keepdims=True) / members
    state_pert = jnp.where(real, states - state_mean, 0.0).astype(BF16)

    out_copies = []
    if n == 4:
        dests = [turn(3, 3), turn(2, 3), turn(other, 3)]
    else:
        dests = [peer(d) for d in range(n - 1, 0, -1)]
    for d, dest in enumerate(dests + [me]):
        rows = wt[pl.ds(pl.multiple_of(dest * pad, 16), pad), :]
        result = (state_mean + jnp.dot(rows, state_pert, preferred_element_type=F32))
        result = pack(result, m, oloc.shape[1:])
        if d == n - 1:
            oland[me] = result
        else:
            oloc[d] = result
            out_copies.append(
                send(oloc.at[d], oland.at[me], o_ss.at[d], o_rs.at[me], (dest, col))
            )

    def finish(source):
        out_ref[:, pl.ds(pl.multiple_of(source * cells, 128), cells)] = unpack(oland[source], m, pad, cells)[0:m].astype(BF16)

    finish(me)
    for source in reversed(dests):
        pltpu.make_async_remote_copy(
            src_ref=oloc.at[0], dst_ref=oland.at[source], send_sem=o_ss.at[0], recv_sem=o_rs.at[source],
            device_id=(source, col), device_id_type=MESH,
        ).wait_recv()
        finish(source)
    for copy in obs_copies + state_copies + out_copies:
        copy.wait_send()
    for copy in (w_left, w_right, y_up, y_down, g_right, g_left):
        copy.wait_send()
    if n == 4:
        @pl.when(inner)
        def _():
            for i, (source, slot) in enumerate(handed):
                hand_on(i, source, slot).wait_send()


def local(background, obs_index, yobs, loc_list, loc_count, loc_weight):
    n, regs = lax.axis_size("mem"), lax.axis_size("reg")
    m = background.shape[0]
    rows, width = obs_index.shape[1], obs_index.shape[2]
    cells = background.shape[2] // rows
    length = loc_list.shape[2]
    pad = (m // 16 + 1) * 16
    total = n * pad
    block = -(-3 * (width // 128) // 8) * 8
    obs_block, state_block = packed_shape(m, pad, width), packed_shape(m, pad, cells)
    vmem = pl.BlockSpec(memory_space=pltpu.VMEM)
    dma = pltpu.SemaphoreType.DMA
    result = pl.pallas_call(
        functools.partial(kernel, n, regs, m, pad, width, cells),
        out_shape=jax.ShapeDtypeStruct((m, rows * cells), BF16),
        in_specs=[pl.BlockSpec(memory_space=pltpu.HBM)] * 5 + [pl.BlockSpec(memory_space=pltpu.SMEM)],
        out_specs=vmem,
        scratch_shapes=[
            pltpu.VMEM((m, rows * cells), BF16),
            pltpu.VMEM((rows, width), jnp.int32),
            pltpu.VMEM((1, width), BF16),
            pltpu.VMEM((1, length), jnp.int32),
            pltpu.VMEM((1, length), F32),
            pltpu.VMEM((n, pad, cells), BF16),
            pltpu.VMEM((n, *state_block), BF16),
            pltpu.VMEM((n, *obs_block), BF16),
            pltpu.VMEM((n, 3, *obs_block), BF16),
            pltpu.VMEM((n, *state_block), BF16),
            pltpu.VMEM((3 * block, 128), F32),
            pltpu.VMEM((2, block, 128), F32),
            pltpu.VMEM((8, width), F32),
            pltpu.VMEM((3, 8, width), F32),
            pltpu.VMEM((3, total, total), F32),
            pltpu.VMEM((2, total, total), BF16),
            pltpu.VMEM((2, total, total), BF16),
            pltpu.VMEM((total, total), BF16),
            pltpu.VMEM((n, *state_block), BF16),
            pltpu.VMEM((n, *state_block), BF16),
            dma((3 * n,)), dma((n, 3)),
            dma((n,)), dma((n,)),
            dma((2,)), dma((2,)),
            dma((2,)), dma((2,)),
            dma((2,)), dma((2,)),
            dma((n,)), dma((n,)), dma((5,)),
        ],
        compiler_params=pltpu.CompilerParams(
            collective_id=0, has_side_effects=True, vmem_limit_bytes=40 * 1024 * 1024
        ),
    )(
        *(
            pltpu.with_memory_space_constraint(x, pltpu.HBM)
            for x in (
                background.reshape(m, rows * cells),
                obs_index.reshape(rows, width),
                yobs.reshape(1, width),
                loc_list.reshape(1, length),
                loc_weight.reshape(1, length),
            )
        ),
        loc_count.reshape(1, 1),
    )
    return result.reshape(m, 1, rows * cells)


def solution(mesh):
    return jax.shard_map(
        local,
        mesh=mesh,
        in_specs=(
            P("mem", "reg", None),
            P("reg", None, None),
            P("reg", "mem", None),
            P("reg", "mem", None),
            P("reg", "mem"),
            P("reg", "mem", None),
        ),
        out_specs=P("mem", "reg", None),
        check_vma=False,
    )
```

```python
import functools
import math

import jax
import jax.numpy as jnp
from jax import lax
from jax.experimental import pallas as pl
from jax.experimental.pallas import tpu as pltpu
from jax.sharding import PartitionSpec as P

NS_STEPS = 5
INFLATION = 1.1
MESH = pl.DeviceIdType.MESH
F32 = jnp.float32
BF16 = jnp.bfloat16


def split(x):
    high = x.astype(BF16)
    return high, (x - high.astype(F32)).astype(BF16)


def mm(a, b, passes):
    top = jnp.dot(a[0], b[0], preferred_element_type=F32)
    if passes == 1:
        return top
    return (
        jnp.dot(a[0], b[1], preferred_element_type=F32)
        + jnp.dot(a[1], b[0], preferred_element_type=F32)
        + top
    )


def dot_t(a, b):
    return lax.dot_general(a, b, (((1,), (1,)), ((), ())), preferred_element_type=F32)


def newton(gram, norm, eye, steps):
    t = gram * (1.0 / norm)
    root = None
    for step in range(steps):
        passes = 1 if step < steps - 2 else 3
        t_s = split(t)
        if root is None:
            root = 1.5 * eye - 0.5 * t
        else:
            root = 1.5 * root - 0.5 * mm(t_s, split(root), passes)
        if step < steps - 1:
            square = mm(t_s, t_s, passes)
            t = 2.25 * t - 1.5 * square + 0.25 * mm(t_s, split(square), passes)
    return root


def packed_shape(m, pad, width):
    rest = m % 16
    base = m - rest
    if rest and base and base % rest == 0 and (width * rest // base) % 128 == 0 and width * rest % base == 0:
        return base, width + width * rest // base
    return pad, width


def pack(x, m, shape):
    base, lanes = shape
    width = x.shape[1]
    if lanes == width:
        return x.astype(BF16)
    extra = lanes - width
    rest = jnp.concatenate([x[base:m, i:i + extra] for i in range(0, width, extra)], axis=0)
    return jnp.concatenate([x[:base], rest], axis=1).astype(BF16)


def unpack(y, m, pad, width):
    y = y.astype(F32)
    if y.shape[1] == width:
        return y
    rest = m - y.shape[0]
    tail = jnp.concatenate([y[i:i + rest, width:] for i in range(0, y.shape[0], rest)], axis=1)
    return jnp.concatenate([y[:, :width], tail, jnp.zeros((pad - m, width), F32)], axis=0)


def kernel(
    n, regs, m, pad, width, cells,
    bg_hbm, idx_hbm, yobs_hbm, list_hbm, weight_hbm, count_ref,
    out_ref,
    bg_ref, idx_ref, yobs_ref, list_ref, weight_ref,
    bgp, spack, obs_loc, obuf, sbuf, wd, wbuf, yloc, ybuf, gacc, gsend, grecv, wt, oloc, oland,
    obs_ss, obs_rs, st_ss, st_rs, w_ss, w_rs, y_ss, y_rs, g_ss, g_rs, o_ss, o_rs, in_sem,
):
    me, col = lax.axis_index("mem"), lax.axis_index("reg")
    left, right = lax.rem(col + regs - 1, regs), lax.rem(col + 1, regs)
    members, total = n * m, n * pad
    lanes = 128
    strips = width // lanes
    block = wd.shape[0] // 3

    def peer(d):
        return lax.rem(me + d, n)

    barrier = pltpu.get_barrier_semaphore()
    for d in range(1, n):
        pl.semaphore_signal(barrier, inc=1, device_id=(peer(d), col), device_id_type=MESH)
    for c in (left, right):
        pl.semaphore_signal(barrier, inc=1, device_id=(me, c), device_id_type=MESH)

    def send(src, dst, ss, rs, device):
        copy = pltpu.make_async_remote_copy(
            src_ref=src, dst_ref=dst, send_sem=ss, recv_sem=rs,
            device_id=device, device_id_type=MESH,
        )
        copy.start()
        return copy

    loads = [
        pltpu.make_async_copy(src, dst, in_sem.at[i])
        for i, (src, dst) in enumerate((
            (bg_hbm, bg_ref), (idx_hbm, idx_ref), (yobs_hbm, yobs_ref),
            (list_hbm, list_ref), (weight_hbm, weight_ref),
        ))
    ]
    for load in loads:
        load.start()

    for load in loads[:3]:
        load.wait()
    tail = (m // 16) * 16
    for q in range(n):
        bgp[q, tail:pad, :] = jnp.zeros((pad - tail, cells), BF16)
        bgp[q, 0:m, :] = bg_ref[:, q * cells:(q + 1) * cells]

    yloc[...] = jnp.broadcast_to(yobs_ref[...].astype(F32), yloc.shape)
    ybuf[1] = yloc[...]

    pl.semaphore_wait(barrier, n + 1)

    y_up = send(yloc, ybuf.at[0], y_ss.at[0], y_rs.at[0], (peer(1), col))
    y_down = send(yloc, ybuf.at[2], y_ss.at[1], y_rs.at[1], (peer(n - 1), col))

    def observe(row):
        hot = lax.broadcasted_iota(jnp.int32, (cells, width), 0) == idx_ref[pl.ds(row, 1), :]
        hot = jnp.where(hot, 1.0, 0.0).astype(BF16)
        seen = jnp.dot(bgp[row], hot, preferred_element_type=F32)
        return pack(seen, m, obs_loc.shape[1:])

    obs_copies = []
    if n == 4:
        side = me // 2

        def turn(x, last):
            return x + side * (last - 2 * x)

        here = turn(me, 3)
        inner = here == 1
        other = 1 - here

        def obs_send(row, dest, slot, i):
            return send(
                obs_loc.at[row], obuf.at[me, turn(slot, 2)], obs_ss.at[i],
                obs_rs.at[me, turn(slot, 2)], (turn(dest, 3), col),
            )

        def landed(source, slot):
            return pltpu.make_async_remote_copy(
                src_ref=obs_loc.at[0], dst_ref=obuf.at[turn(source, 3), turn(slot, 2)],
                send_sem=obs_ss.at[0], recv_sem=obs_rs.at[turn(source, 3), turn(slot, 2)],
                device_id=(turn(other, 3), col), device_id_type=MESH,
            )

        for i, (row, dest, slot) in enumerate(((2, 2, 1), (3, 2, 2), (1, 2, 0), (0, 3, 2))):
            obs_loc[row] = observe(turn(row, 3))
            obs_copies.append(obs_send(row, dest, slot, i))
        def kth(place, k):
            return (2 - place, 1 - place, 2 * place)[k]

        for k in range(3):
            slot = kth(other, k)
            obs_copies.append(obs_send(lax.rem(other + slot + 3, 4), other, slot, 4 + k))
        for slot in range(3):
            obuf[me, turn(slot, 2)] = obs_loc[lax.rem(here + slot + 3, 4)]

        handed = ((2, 1), (2, 0), (3, 1), (3, 0))

        def hand_on(i, source, slot):
            return pltpu.make_async_remote_copy(
                src_ref=obuf.at[turn(source, 3), turn(slot, 2)],
                dst_ref=obuf.at[turn(source, 3), turn(slot + 1, 2)],
                send_sem=obs_ss.at[7 + i], recv_sem=obs_rs.at[turn(source, 3), turn(slot + 1, 2)],
                device_id=(turn(0, 3), col), device_id_type=MESH,
            )
    else:
        for t in sorted(range(n), key=lambda t: -min(t, n - t)):
            obs_loc[t] = observe(peer(t))
            for slot in (0, 1, 2):
                d = (t + 1 - slot) % n
                if d == 0:
                    obuf[me, slot] = obs_loc[t]
                else:
                    obs_copies.append(
                        send(
                            obs_loc.at[t], obuf.at[me, slot], obs_ss.at[3 * d + slot],
                            obs_rs.at[d, slot], (peer(d), col),
                        )
                    )

    for load in loads[3:]:
        load.wait()
    length = list_ref.shape[1]
    place = lax.broadcasted_iota(jnp.int32, (1, length), 1)
    live = jnp.where(place < count_ref[0, 0], weight_ref[...], 0.0)
    part0 = live.astype(BF16)
    rest = live - part0.astype(F32)
    part1 = rest.astype(BF16)
    part2 = (rest - part1.astype(F32)).astype(BF16)
    cand = list_ref[...]
    strip = cand // lanes
    lane = cand - strip * lanes
    group = strip // (3 * strips)
    strip = strip + group * (block - 3 * strips)
    rows_at = lax.broadcasted_iota(jnp.int32, (3 * block, length), 0) == strip
    lanes_at = lax.broadcasted_iota(jnp.int32, (lanes, length), 0) == lane
    lane_hot = jnp.where(lanes_at, 1.0, 0.0).astype(BF16)
    spread = [
        dot_t(jnp.where(rows_at, part.astype(F32), 0.0).astype(BF16), lane_hot)
        for part in (part0, part1, part2)
    ]
    wd[...] = spread[0] + (spread[1] + spread[2])
    w_left = send(wd.at[pl.ds(0, block)], wbuf.at[0], w_ss.at[0], w_rs.at[0], (me, left))
    w_right = send(wd.at[pl.ds(2 * block, block)], wbuf.at[1], w_ss.at[1], w_rs.at[1], (me, right))

    def state_send(dest, i):
        return send(spack.at[dest], sbuf.at[me], st_ss.at[i], st_rs.at[me], (dest, col))

    for q in range(n):
        spack[q] = pack(bgp[q].astype(F32), m, spack.shape[1:])
    sbuf[me] = spack[me]
    if n == 4:
        state_copies = [state_send(turn(2, 3), 0)]
        state_later = [turn(3, 3), turn(other, 3)]
    else:
        state_copies = []
        state_later = [peer(d) for d in range(n - 1, 0, -1)]

    if n == 4:
        @pl.when(inner)
        def _():
            for i, (source, slot) in enumerate(handed):
                landed(source, slot).wait_recv()
                hand_on(i, source, slot).start()

    for dest in state_later:
        state_copies.append(state_send(dest, len(state_copies)))

    def take(k):
        if n != 4:
            if k == 0:
                for copy in obs_copies:
                    copy.wait_recv()
            return k
        slot = kth(here, k)
        if k == 2:
            for source in (2, 3):
                landed(source, slot).wait_recv()
        else:
            @pl.when(jnp.logical_not(inner))
            def _():
                for source in (2, 3):
                    landed(source, slot).wait_recv()
        landed(other, slot).wait_recv()
        return turn(slot, 2)

    row_id = lax.broadcasted_iota(jnp.int32, (total, 1), 0)
    real = lax.rem(row_id, pad) < m

    def perturbed(slot):
        seen = jnp.concatenate([unpack(obuf[z, slot], m, pad, width) for z in range(n)], axis=0)
        mean = jnp.sum(seen, axis=0, keepdims=True) / members
        innov = ybuf[slot][0:1, :] - mean
        values = jnp.where(real, seen - mean, jnp.where(row_id == m, innov, 0.0))
        return values.astype(BF16)

    def term(values, weights, slot):
        strip_rows = [weights[pl.ds(slot * strips + i, 1), :] for i in range(strips)]
        scale = jnp.concatenate(strip_rows, axis=1)
        return dot_t((values.astype(F32) * scale).astype(BF16), values)

    tables = (wbuf.at[0], wbuf.at[1], wd.at[pl.ds(block, block)])
    for k in range(2):
        slot = take(k)
        if k == 0:
            for copy in (y_up, y_down, w_left, w_right):
                copy.wait_recv()
        values = perturbed(slot)
        for i, table in enumerate(tables):
            if k == 0:
                gacc[i] = term(values, table, slot)
            else:
                gacc[i] += term(values, table, slot)
    slot = take(2)

    values = perturbed(slot)
    gsend[0] = (gacc[0] + term(values, tables[0], slot)).astype(BF16)
    g_right = send(gsend.at[0], grecv.at[0], g_ss.at[0], g_rs.at[0], (me, right))
    gsend[1] = (gacc[1] + term(values, tables[1], slot)).astype(BF16)
    g_left = send(gsend.at[1], grecv.at[1], g_ss.at[1], g_rs.at[1], (me, left))
    own = gacc[2] + term(values, tables[2], slot)
    g_right.wait_recv()
    g_left.wait_recv()
    full = own + (grecv[0].astype(F32) + grecv[1].astype(F32))

    col_id = lax.broadcasted_iota(jnp.int32, (1, total), 1)
    real_col = lax.rem(col_id, pad) < m
    same = row_id == col_id
    eye = jnp.where(same, 1.0, 0.0)
    drive = jnp.where(real_col, full[m:m + 1, :], 0.0)
    gram = jnp.where(real & real_col, full, 0.0)
    gram = gram + jnp.where(same & real, (members - 1) / INFLATION, 0.0)
    norm = jnp.sqrt(jnp.sum(jnp.sum(gram * gram, axis=0, keepdims=True), axis=1, keepdims=True))
    root = newton(gram, norm, eye, NS_STEPS)
    product = jnp.sum(root * drive, axis=1, keepdims=True)
    shift = jnp.sum(root * product, axis=0, keepdims=True)
    wt[...] = (math.sqrt(members - 1) / jnp.sqrt(norm) * root + shift / norm).astype(BF16)

    for d in range(1, n):
        pltpu.make_async_remote_copy(
            src_ref=spack.at[0], dst_ref=sbuf.at[peer(d)], send_sem=st_ss.at[0], recv_sem=st_rs.at[peer(d)],
            device_id=(peer(d), col), device_id_type=MESH,
        ).wait_recv()
    states = jnp.concatenate([unpack(sbuf[z], m, pad, cells) for z in range(n)], axis=0)
    state_mean = jnp.sum(states, axis=0, keepdims=True) / members
    state_pert = jnp.where(real, states - state_mean, 0.0).astype(BF16)

    out_copies = []
    if n == 4:
        dests = [turn(3, 3), turn(2, 3), turn(other, 3)]
    else:
        dests = [peer(d) for d in range(n - 1, 0, -1)]
    for d, dest in enumerate(dests + [me]):
        rows = wt[pl.ds(pl.multiple_of(dest * pad, 16), pad), :]
        result = (state_mean + jnp.dot(rows, state_pert, preferred_element_type=F32))
        result = pack(result, m, oloc.shape[1:])
        if d == n - 1:
            oland[me] = result
        else:
            oloc[d] = result
            out_copies.append(
                send(oloc.at[d], oland.at[me], o_ss.at[d], o_rs.at[me], (dest, col))
            )

    def finish(source):
        out_ref[:, pl.ds(pl.multiple_of(source * cells, 128), cells)] = unpack(oland[source], m, pad, cells)[0:m].astype(BF16)

    finish(me)
    for source in reversed(dests):
        pltpu.make_async_remote_copy(
            src_ref=oloc.at[0], dst_ref=oland.at[source], send_sem=o_ss.at[0], recv_sem=o_rs.at[source],
            device_id=(source, col), device_id_type=MESH,
        ).wait_recv()
        finish(source)
    for copy in obs_copies + state_copies + out_copies:
        copy.wait_send()
    for copy in (w_left, w_right, y_up, y_down, g_right, g_left):
        copy.wait_send()
    if n == 4:
        @pl.when(inner)
        def _():
            for i, (source, slot) in enumerate(handed):
                hand_on(i, source, slot).wait_send()


def local(background, obs_index, yobs, loc_list, loc_count, loc_weight):
    n, regs = lax.axis_size("mem"), lax.axis_size("reg")
    m = background.shape[0]
    rows, width = obs_index.shape[1], obs_index.shape[2]
    cells = background.shape[2] // rows
    length = loc_list.shape[2]
    pad = (m // 16 + 1) * 16
    total = n * pad
    block = -(-3 * (width // 128) // 8) * 8
    obs_block, state_block = packed_shape(m, pad, width), packed_shape(m, pad, cells)
    vmem = pl.BlockSpec(memory_space=pltpu.VMEM)
    dma = pltpu.SemaphoreType.DMA
    result = pl.pallas_call(
        functools.partial(kernel, n, regs, m, pad, width, cells),
        out_shape=jax.ShapeDtypeStruct((m, rows * cells), BF16),
        in_specs=[pl.BlockSpec(memory_space=pltpu.HBM)] * 5 + [pl.BlockSpec(memory_space=pltpu.SMEM)],
        out_specs=vmem,
        scratch_shapes=[
            pltpu.VMEM((m, rows * cells), BF16),
            pltpu.VMEM((rows, width), jnp.int32),
            pltpu.VMEM((1, width), BF16),
            pltpu.VMEM((1, length), jnp.int32),
            pltpu.VMEM((1, length), F32),
            pltpu.VMEM((n, pad, cells), BF16),
            pltpu.VMEM((n, *state_block), BF16),
            pltpu.VMEM((n, *obs_block), BF16),
            pltpu.VMEM((n, 3, *obs_block), BF16),
            pltpu.VMEM((n, *state_block), BF16),
            pltpu.VMEM((3 * block, 128), F32),
            pltpu.VMEM((2, block, 128), F32),
            pltpu.VMEM((8, width), F32),
            pltpu.VMEM((3, 8, width), F32),
            pltpu.VMEM((3, total, total), F32),
            pltpu.VMEM((2, total, total), BF16),
            pltpu.VMEM((2, total, total), BF16),
            pltpu.VMEM((total, total), BF16),
            pltpu.VMEM((n, *state_block), BF16),
            pltpu.VMEM((n, *state_block), BF16),
            dma((3 * n,)), dma((n, 3)),
            dma((n,)), dma((n,)),
            dma((2,)), dma((2,)),
            dma((2,)), dma((2,)),
            dma((2,)), dma((2,)),
            dma((n,)), dma((n,)), dma((5,)),
        ],
        compiler_params=pltpu.CompilerParams(
            collective_id=0, has_side_effects=True, vmem_limit_bytes=40 * 1024 * 1024
        ),
    )(
        *(
            pltpu.with_memory_space_constraint(x, pltpu.HBM)
            for x in (
                background.reshape(m, rows * cells),
                obs_index.reshape(rows, width),
                yobs.reshape(1, width),
                loc_list.reshape(1, length),
                loc_weight.reshape(1, length),
            )
        ),
        loc_count.reshape(1, 1),
    )
    return result.reshape(m, 1, rows * cells)


def solution(mesh):
    return jax.shard_map(
        local,
        mesh=mesh,
        in_specs=(
            P("mem", "reg", None),
            P("reg", None, None),
            P("reg", "mem", None),
            P("reg", "mem", None),
            P("reg", "mem"),
            P("reg", "mem", None),
        ),
        out_specs=P("mem", "reg", None),
        check_vma=False,
    )
```
